512 devices in a mesh: dp: 64 (over y, x, core), proto: 8 (over z).
Axes of the slice: x: 4, y: 8, z: 8, core: 2. Of those that a mesh axis runs over, the one named last changes fastest.
Arguments:
- embeddings: bfloat16 [2, 131072, 128], P(None, ('dp', 'proto')), may hold values from -1 to 1
- prototypes: bfloat16 [128, 4096], P(None, 'proto'), may hold values from -1 to 1
Outputs:
- grad_embed: float32 [2, 131072, 128], P(None, ('dp', 'proto'))
- grad_proto: float32 [128, 4096], P(None, 'proto')
The draws below stay inside these ranges and needn't reach their ends.
All inputs are finite; a program needn't handle non-finite values.
Results may differ from the reference program's by a relative error of at most 0.02.
Values may be sent and summed in bfloat16 or wider, within the bound.
No kernel may reach another device: no remote copies, remote signals or barrier semaphores. Data moves between devices by JAX's collectives and lax.ppermute only.
A program may use at most 64 MiB of HBM per device.

```python
import math
import jax
import jax.numpy as jnp
from jax import lax

D = 128
K = 4096
U_DEV = 256
ITERS = 3
USERS = 131072
N_PROTO = 8


def common_directions(key):
    return jax.random.normal(key, (N_PROTO + 1, D), jnp.float32) / math.sqrt(D)


def draw_embeddings(key, part):
    directions = common_directions(key)
    key = jax.random.fold_in(key, 5)
    subkeys = jax.random.split(key, 8)
    block_rows = U_DEV * N_PROTO
    block_count = USERS // block_rows
    base_rows = jax.random.normal(subkeys[0], (USERS, D), jnp.float32) / math.sqrt(D)
    view_noise = jax.random.normal(subkeys[1], (2, USERS, D), jnp.float32) / math.sqrt(D)
    level_low, level_high, favored_weight, scale_low, scale_high = (0.3, 0.6, 0.7, 0.7, 1.4)
    block_signs = jnp.where(jax.random.bernoulli(subkeys[2], 0.5, (block_count,)), 1.0, -1.0)
    levels = block_signs * jax.random.uniform(subkeys[3], (block_count,), jnp.float32, level_low, level_high)
    user_level = jnp.repeat(levels, block_rows) + 0.15 * jax.random.normal(subkeys[4], (USERS,), jnp.float32)
    favorite = jax.random.randint(subkeys[5], (USERS,), 0, N_PROTO)
    extra_terms = 0.12 * jax.random.normal(subkeys[6], (USERS, N_PROTO), jnp.float32)
    shard_ids = jnp.arange(N_PROTO, dtype=jnp.int32)
    coefficients = extra_terms + favored_weight * (favorite[:, None] == shard_ids[None, :]).astype(jnp.float32)
    vectors = base_rows[None] + 0.6 * view_noise + user_level[None, :, None] * directions[0][None, None, :]
    for column_shard in range(N_PROTO):
        vectors = vectors + coefficients[None, :, column_shard:column_shard + 1] * directions[1 + column_shard][None, None, :]
    row_scale = jnp.exp(jax.random.uniform(subkeys[7], (2, USERS, 1), jnp.float32, math.log(scale_low), math.log(scale_high)))
    return jnp.clip(vectors * 0.7 * row_scale, -1.0, 1.0).astype(jnp.bfloat16)


def draw_prototypes(key, part):
    directions = common_directions(key)
    key = jax.random.fold_in(key, 9)
    subkeys = jax.random.split(key, 4)
    base_cols = jax.random.normal(subkeys[0], (D, K), jnp.float32) / math.sqrt(D)
    affinity_level, affinity_slope, global_spread = (0.4, 0.4, 0.5)
    per_shard = K // N_PROTO
    owner = jnp.arange(K, dtype=jnp.int32) // per_shard
    shard_dirs = jnp.take(directions, owner + 1, axis=0).T
    affinity = affinity_level + jax.random.uniform(subkeys[1], (K,), jnp.float32, -affinity_slope, affinity_slope)
    global_coef = jax.random.uniform(subkeys[2], (K,), jnp.float32, -global_spread, global_spread)
    columns = base_cols + affinity[None, :] * shard_dirs + global_coef[None, :] * directions[0][:, None]
    column_scale = jnp.exp(jax.random.uniform(subkeys[3], (1, K), jnp.float32, math.log(0.5), math.log(2.0)))
    return jnp.clip(columns * column_scale, -1.0, 1.0).astype(jnp.bfloat16)


def setup_inputs(seed: int = 0) -> dict:
    key_of = jax.random.split(jax.random.key(seed), 3)
    embeddings = draw_embeddings(jax.random.fold_in(key_of[2], 71), 0)
    prototypes = draw_prototypes(jax.random.fold_in(key_of[2], 71), 0)
    return dict(embeddings=embeddings, prototypes=prototypes)


sink_eps = 0.05
sharpness_divisor = 0.1

def reference(embeddings, prototypes):
    floats = embeddings.astype(jnp.float32)
    inverse = lax.rsqrt(lax.optimization_barrier(jnp.sum(floats * floats, -1, keepdims=True)) + 1e-06)
    unit_rows = floats * inverse
    normed_halfprecision = unit_rows.astype(jnp.bfloat16)
    proto_f = prototypes.astype(jnp.float32)
    unit_proto = (proto_f * lax.rsqrt(lax.optimization_barrier(jnp.sum(proto_f * proto_f, 0, keepdims=True)) + 1e-06)).astype(jnp.bfloat16)
    proto_wide = unit_proto.astype(jnp.float32)
    block_rows = U_DEV * N_PROTO
    blocks = normed_halfprecision.reshape(2, USERS // block_rows, block_rows, D).transpose(1, 0, 2, 3)

    def scored(user_block):
        return jnp.einsum('vrd,dk->vrk', user_block.astype(jnp.float32), proto_wide)

    def first_mass(total, user_block):
        kernel = jnp.exp(scored(user_block) / sink_eps)
        return (total + lax.optimization_barrier(jnp.sum(kernel, 1)), None)
    col_total, _ = lax.scan(first_mass, jnp.zeros((2, K), jnp.float32), blocks)
    col_scale = 1.0 / (K * col_total)
    for sweep in range(ITERS - 1):

        def next_mass(total, user_block, col_scale=col_scale):
            kernel = jnp.exp(scored(user_block) / sink_eps)
            row_sum_value = lax.optimization_barrier(jnp.sum(kernel * col_scale[:, None, :], 2))
            row_scale = 1.0 / (USERS * row_sum_value)
            return (total + lax.optimization_barrier(jnp.sum(kernel * row_scale[:, :, None], 1)), None)
        col_total, _ = lax.scan(next_mass, jnp.zeros((2, K), jnp.float32), blocks)
        col_scale = 1.0 / (K * col_total)

    def gradients(total, user_block):
        raw_similarity = scored(user_block)
        kernel = jnp.exp(raw_similarity / sink_eps)
        weighted = kernel * col_scale[:, None, :]
        cluster_labels = weighted / lax.optimization_barrier(jnp.sum(weighted, 2, keepdims=True))
        powered_entries = jnp.exp(raw_similarity / sharpness_divisor)
        likelihood_matrix = powered_entries / lax.optimization_barrier(jnp.sum(powered_entries, 2, keepdims=True))
        similarity_slope = ((likelihood_matrix - cluster_labels[::-1]) / sharpness_divisor).astype(jnp.bfloat16).astype(jnp.float32)
        grad_unit = jnp.einsum('vrk,dk->vrd', similarity_slope, proto_wide)
        total = total + jnp.einsum('vrd,vrk->dk', user_block.astype(jnp.float32), similarity_slope)
        return (total, grad_unit)
    grad_proto, grad_unit = lax.scan(gradients, jnp.zeros((D, K), jnp.float32), blocks)
    grad_unit = grad_unit.transpose(1, 0, 2, 3).reshape(2, USERS, D)
    grad_embed = inverse * (grad_unit - unit_rows * lax.optimization_barrier(jnp.sum(unit_rows * grad_unit, -1, keepdims=True)))
    return (grad_embed, grad_proto)
```

```python
import jax
import jax.numpy as jnp
from jax import lax
from jax.sharding import PartitionSpec as P

K = 4096
ITERS = 3


sink_eps = 0.05
sharpness_divisor = 0.1


def share(x, axis):
    n = lax.axis_size(axis)
    return lax.all_to_all(jnp.broadcast_to(x[None], (n, *x.shape)), axis, 0, 0)


def total(x, axis):
    return jnp.sum(share(x, axis), 0)


def body(embeddings, prototypes):
    floats = embeddings.astype(jnp.float32)
    inverse = lax.rsqrt(jnp.sum(floats * floats, -1, keepdims=True) + 1e-06)
    unit_rows = floats * inverse
    normed_halfprecision = unit_rows.astype(jnp.bfloat16)
    proto_f = prototypes.astype(jnp.float32)
    unit_proto = (proto_f * lax.rsqrt(jnp.sum(proto_f * proto_f, 0, keepdims=True) + 1e-06)).astype(
        jnp.bfloat16
    )
    own_rows = embeddings.shape[1]
    n_dp, n_proto = lax.axis_size("dp"), lax.axis_size("proto")
    users_all = own_rows * n_dp * n_proto
    group_rows = share(normed_halfprecision, "proto")
    raw_similarity = jnp.einsum(
        "gvrd,dk->vgrk", group_rows, unit_proto, preferred_element_type=jnp.float32
    )
    kernel = jnp.exp(raw_similarity / sink_eps)
    powered_entries = jnp.exp(raw_similarity / sharpness_divisor)
    soft_partial = jnp.sum(powered_entries, 3)
    col_scale = 1.0 / (K * total(jnp.sum(kernel, (1, 2)), "dp"))
    first_partial = jnp.einsum("vgrk,vk->vgr", kernel, col_scale)
    row_sum_value, soft_total = total(jnp.stack([first_partial, soft_partial]), "proto")
    for sweep in range(ITERS - 1):
        row_scale = 1.0 / (users_all * row_sum_value)
        col_scale = 1.0 / (K * total(jnp.einsum("vgrk,vgr->vk", kernel, row_scale), "dp"))
        row_sum_value = total(jnp.einsum("vgrk,vk->vgr", kernel, col_scale), "proto")
    cluster_labels = kernel * col_scale[:, None, None, :] / row_sum_value[..., None]
    likelihood_matrix = powered_entries / soft_total[..., None]
    similarity_slope = ((likelihood_matrix - cluster_labels[::-1]) / sharpness_divisor).astype(
        jnp.bfloat16
    )
    unit_part = jnp.einsum(
        "vgrk,dk->gvrd", similarity_slope, unit_proto, preferred_element_type=jnp.float32
    ).astype(jnp.bfloat16)
    grad_unit = jnp.sum(lax.all_to_all(unit_part, "proto", 0, 0).astype(jnp.float32), 0)
    grad_part = jnp.einsum(
        "gvrd,vgrk->dk", group_rows, similarity_slope, preferred_element_type=jnp.float32
    )
    pieces = grad_part.reshape(n_dp, -1, 512)
    grad_proto = share(jnp.sum(lax.all_to_all(pieces, "dp", 0, 0), 0), "dp").reshape(grad_part.shape)
    grad_embed = inverse * (
        grad_unit - unit_rows * jnp.sum(unit_rows * grad_unit, -1, keepdims=True)
    )
    return (grad_embed, grad_proto)


def solution(mesh):
    placed = (P(None, ("dp", "proto"), None), P(None, "proto"))
    return jax.shard_map(
        body,
        mesh=mesh,
        in_specs=placed,
        out_specs=(P(None, ("dp", "proto"), None), P(None, "proto")),
        check_vma=False,
    )
```

```python
import functools

import jax
import jax.numpy as jnp
from jax import lax
from jax.experimental import pallas as pl
from jax.experimental.pallas import tpu as pltpu
from jax.sharding import Mesh, PartitionSpec as P

K = 4096
ITERS = 3
SINK = 0.05
SHARP = 0.1

NY, NX, NC, NZ = 8, 4, 2, 8
G = NX * NC
U = 256
SUB = 512 // G
COLS = NZ * SUB
Q = COLS // 128
f32, bf16 = jnp.float32, jnp.bfloat16
VM = pl.BlockSpec(memory_space=pltpu.VMEM)


def call(kernel, outs, *args):
    return pl.pallas_call(
        kernel,
        out_shape=outs,
        in_specs=[VM] * len(args),
        out_specs=jax.tree.map(lambda _: VM, outs),
        compiler_params=pltpu.CompilerParams(vmem_limit_bytes=20 * 1024 * 1024),
    )(*args)


def fold(x):
    return jnp.sum(x.reshape(-1, 8, x.shape[-1]), 0)


def send_columns(acc, out):
    rows = [jnp.sum(acc[i].T, 0, keepdims=True) for i in range(2 * Q)]
    part = jnp.concatenate(rows, 0)
    out[...] = jnp.concatenate([part] * (NY * NZ), 0).astype(out.dtype)


def groups(step, mine, other):
    core = lax.axis_index("c")
    for half, rows in enumerate((mine, other)):
        def member(x, _):
            step(lax.rem(core + half, NC) * NX + x, x, rows)
            return 0

        lax.fori_loop(0, NX, member, 0)


def scores_kernel(mine, other, proto, powered, masses, soft, columns, acc):
    acc[...] = jnp.zeros_like(acc)

    def group(g, x, rows):
        for v in range(2):
            rowsum = jnp.zeros((8, U), f32)
            for q in range(Q):
                s = lax.dot_general(
                    proto[q * 128 : (q + 1) * 128, :],
                    rows[x, v],
                    (((1,), (1,)), ((), ())),
                    preferred_element_type=f32,
                )
                e = jnp.exp(s * (1.0 / SHARP))
                k = e * e
                powered[g, v, q * 128 : (q + 1) * 128, :] = e
                masses[g, v, q * 128 : (q + 1) * 128, :] = k
                rowsum += fold(e)
                acc[v * Q + q] += k[:, :128] + k[:, 128:]
            soft[g, v : v + 1, :] = jnp.sum(rowsum, 0, keepdims=True)

    groups(group, mine, other)
    send_columns(acc, columns)


def rows_kernel(with_soft, masses, columns, *refs):
    soft, (out, scale) = (refs[0], refs[1:]) if with_soft else (None, refs)
    got = columns[...].astype(f32)
    c = 1.0 / (K * fold(got))
    scale[...] = c
    turned = jnp.concatenate([c] * 16, 0).T
    n = 4 if with_soft else 2

    def group(g, _):
        lines = []
        for v in range(2):
            total = jnp.zeros((8, U), f32)
            for q in range(Q):
                i = v * Q + q
                total += fold(masses[g, v, q * 128 : (q + 1) * 128, :] * turned[:, i : i + 1])
            lines.append(jnp.sum(total, 0, keepdims=True))
        for v in range(2):
            out[0, g, v : v + 1, :] = lines[v]
        if with_soft:
            out[0, g, 2:4, :] = soft[g]
        return 0

    lax.fori_loop(0, G, group, 0)
    for i in range(1, G):
        out[i] = out[0]


def columns_kernel(masses, rowmass, columns, acc):
    acc[...] = jnp.zeros_like(acc)

    def group(g, _):
        total = rowmass[0, g, 0:2, :]
        for i in range(1, G):
            total += rowmass[i, g, 0:2, :]
        r = 1.0 / (NY * NX * NC * NZ * U * total)
        for v in range(2):
            for q in range(Q):
                k = masses[g, v, q * 128 : (q + 1) * 128, :] * r[v : v + 1, :]
                acc[v * Q + q] += k[:, :128] + k[:, 128:]
        return 0

    lax.fori_loop(0, G, group, 0)
    send_columns(acc, columns)


def slopes_kernel(mine, other, proto, powered, masses, scale, first, last, unit, parts, acc):
    acc[...] = jnp.zeros_like(acc)
    turned = jnp.concatenate([scale[...] * (1.0 / SHARP)] * 16, 0).T

    def group(g, x, rows):
        soft, mass = first[0, g, 2:4, :], last[0, g, 0:2, :]
        for i in range(1, G):
            soft += first[i, g, 2:4, :]
            mass += last[i, g, 0:2, :]
        a = (1.0 / SHARP) / soft
        b = 1.0 / mass
        place = lax.rem(g, NX) * NC + lax.div(g, NX)
        for v in range(2):
            w = 1 - v
            made = jnp.zeros((U, 128), f32)
            for q in range(Q):
                at = slice(q * 128, (q + 1) * 128)
                i = w * Q + q
                slope = (
                    powered[g, v, at, :] * a[v : v + 1, :]
                    - masses[g, w, at, :] * turned[:, i : i + 1] * b[w : w + 1, :]
                ).astype(bf16)
                made += lax.dot_general(
                    slope, proto[at, :], (((0,), (0,)), ((), ())), preferred_element_type=f32
                )
                acc[at, :] += jnp.dot(slope, rows[x, v], preferred_element_type=f32)
            unit[place, v] = made.astype(bf16)

    groups(group, mine, other)
    parts[...] = acc[...].astype(bf16)


def share(x, axis):
    n = lax.axis_size(axis)
    return lax.all_to_all(jnp.broadcast_to(x[None], (n, *x.shape)), axis, 0, 0)


def body(embeddings, prototypes):
    floats = embeddings.astype(f32)
    inverse = lax.rsqrt(jnp.sum(floats * floats, -1, keepdims=True) + 1e-06)
    unit_rows = floats * inverse
    j = lax.axis_index("x") * NC + lax.axis_index("c")
    proto_f = lax.dynamic_slice(prototypes, (0, j * SUB), (128, SUB)).astype(f32).T
    proto_own = (proto_f * lax.rsqrt(jnp.sum(proto_f * proto_f, 1, keepdims=True) + 1e-06)).astype(bf16)
    proto = share(proto_own, "z").reshape(COLS, 128)
    mine = share(unit_rows.astype(bf16), "x")
    other = lax.ppermute(mine, "c", [(0, 1), (1, 0)])

    kept = pltpu.VMEM((G, 2, COLS, U), f32)
    sums = jax.ShapeDtypeStruct((NY * NZ * 8, 128), bf16)
    acc = pltpu.VMEM((2 * Q, 128, 128), f32)

    def with_acc(kernel, outs, *args, scratch=acc):
        return pl.pallas_call(
            kernel,
            out_shape=outs,
            in_specs=[VM] * len(args),
            out_specs=jax.tree.map(lambda _: VM, outs),
            scratch_shapes=[scratch],
            compiler_params=pltpu.CompilerParams(vmem_limit_bytes=20 * 1024 * 1024),
        )(*args)

    powered, masses, soft, columns = with_acc(
        scores_kernel, (kept, kept, jax.ShapeDtypeStruct((G, 2, U), f32), sums), mine, other, proto
    )
    first = None
    for sweep in range(ITERS):
        columns = lax.all_to_all(columns, ("y", "z"), 0, 0, tiled=True)
        more = (soft,) if sweep == 0 else ()
        lines = jax.ShapeDtypeStruct((G, G, 4 if more else 2, U), f32)
        mass, scale = call(
            functools.partial(rows_kernel, bool(more)),
            (lines, jax.ShapeDtypeStruct((8, 128), f32)),
            masses,
            columns,
            *more,
        )
        mass = lax.all_to_all(mass, ("x", "c"), 0, 0)
        first = mass if first is None else first
        if sweep < ITERS - 1:
            columns = with_acc(columns_kernel, sums, masses, mass)
    unit, parts = with_acc(
        slopes_kernel,
        (jax.ShapeDtypeStruct((G, 2, U, 128), bf16), jax.ShapeDtypeStruct((COLS, 128), bf16)),
        mine,
        other,
        proto,
        powered,
        masses,
        scale,
        first,
        mass,
        scratch=pltpu.VMEM((COLS, 128), f32),
    )
    grad_unit = lax.psum_scatter(unit, ("x", "c"), scatter_dimension=0, tiled=True)[0].astype(f32)
    grad_embed = inverse * (
        grad_unit - unit_rows * jnp.sum(unit_rows * grad_unit, -1, keepdims=True)
    )
    pieces = parts.reshape(NZ, NY, SUB // NY, 128).transpose(1, 0, 2, 3)
    pieces = pieces.reshape(NY * NZ, SUB // NY, 128)
    piece = jnp.sum(lax.all_to_all(pieces, ("y", "z"), 0, 0).astype(f32), 0).astype(bf16)
    whole = share(piece, ("y", "x", "c")).reshape(NY, G, SUB // NY, 128).transpose(1, 0, 2, 3)
    grad_proto = whole.reshape(NZ * SUB, 128).astype(f32).T
    return (grad_embed, grad_proto)


def solution(mesh):
    fine = Mesh(mesh.devices.reshape(NY, NX, NC, NZ), ("y", "x", "c", "z"))
    placed = (P(None, ("y", "x", "c", "z"), None), P(None, "z"))
    return jax.shard_map(
        body, mesh=fine, in_specs=placed, out_specs=placed, check_vma=False
    )
```

```python
import functools

import jax
import jax.numpy as jnp
from jax import lax
from jax.experimental import pallas as pl
from jax.experimental.pallas import tpu as pltpu
from jax.sharding import Mesh, PartitionSpec as P

K = 4096
ITERS = 3
SINK = 0.05
SHARP = 0.1

NY, NX, NC, NZ = 8, 4, 2, 8
G = NX * NC
U = 256
SUB = 512 // G
COLS = NZ * SUB
Q = COLS // 128
USERS = NY * NX * NC * NZ * U
EPS = 1e-06
f32, bf16 = jnp.float32, jnp.bfloat16
VM = pl.BlockSpec(memory_space=pltpu.VMEM)
shape = jax.ShapeDtypeStruct


def call(kernel, outs, *args, scratch=()):
    return pl.pallas_call(
        kernel,
        out_shape=outs,
        in_specs=[VM] * len(args),
        out_specs=jax.tree.map(lambda _: VM, outs),
        scratch_shapes=list(scratch),
        compiler_params=pltpu.CompilerParams(vmem_limit_bytes=20 * 1024 * 1024),
    )(*args)


def fold(x):
    return jnp.sum(x.reshape(-1, 8, x.shape[-1]), 0)


def prepare_kernel(embeddings, prototypes, rows, inverse, proto, turned):
    for v in range(2):
        e = embeddings[v].astype(f32)
        inv = lax.rsqrt(jnp.sum(e * e, -1, keepdims=True) + EPS)
        inverse[v] = inv
        unit = (e * inv).astype(bf16)
        for i in range(NX):
            rows[i, v] = unit
    turned[...] = prototypes[...].astype(f32).T
    j = lax.axis_index("x") * NC + lax.axis_index("c")
    own = turned[pl.ds(pl.multiple_of(j * SUB, SUB), SUB), :]
    own = (own * lax.rsqrt(jnp.sum(own * own, -1, keepdims=True) + EPS)).astype(bf16)
    for i in range(NZ):
        proto[i] = own


def send_columns(acc, out):
    rows = [jnp.sum(acc[i * 128 : (i + 1) * 128, :].T, 0, keepdims=True) for i in range(2 * Q)]
    part = jnp.concatenate(rows, 0)
    out[...] = jnp.concatenate([part] * (NY * NZ), 0).astype(out.dtype)


def groups(step, mine, other):
    for half, rows in enumerate((mine, other)):

        def member(x, _):
            step(half, x, rows)
            return 0

        lax.fori_loop(0, NX, member, 0)


def place(half, x):
    return lax.rem(lax.axis_index("c") + half, NC) * NX + x


def scores_kernel(mine, other, proto, powered, masses, soft, columns, acc):
    acc[...] = jnp.zeros_like(acc)

    def group(half, x, rows):
        g = place(half, x)
        for v in range(2):
            rowsum = jnp.zeros((8, U), f32)
            for q in range(Q):
                at = slice(q * 128, (q + 1) * 128)
                s = lax.dot_general(
                    proto[at, :], rows[x, v], (((1,), (1,)), ((), ())), preferred_element_type=f32
                )
                e = jnp.exp(s * (1.0 / SHARP))
                k = e * e
                powered[g, v, at, :] = e.astype(bf16)
                masses[g, v, at, :] = k
                rowsum += fold(e)
                i = v * Q + q
                acc[i * 128 : (i + 1) * 128, :] += k[:, :128] + k[:, 128:]
            soft[pl.ds(v * G + g, 1), :] = jnp.sum(rowsum, 0, keepdims=True)

    groups(group, mine, other)
    send_columns(acc, columns)


def rows_kernel(masses, columns, *refs):
    soft, (out, scale, wide) = (refs[0], refs[1:]) if len(refs) == 4 else (None, refs)
    c = 1.0 / (K * fold(columns[...].astype(f32)))
    scale[...] = c
    turned = jnp.concatenate([c] * 16, 0).T
    for i in range(2 * Q):
        wide[i * 128 : (i + 1) * 128, :] = jnp.broadcast_to(turned[:, i : i + 1], (128, 128))
    lines = []
    for v in range(2):

        def eight(s, acc):
            at = pl.multiple_of(s * 8, 8)
            cc = wide[pl.ds(v * COLS + at, 8), :]
            cc = jnp.concatenate([cc, cc], 1)
            return tuple(acc[g] + masses[g, v, pl.ds(at, 8), :] * cc for g in range(G))

        acc = lax.fori_loop(0, COLS // 8, eight, (jnp.zeros((8, U), f32),) * G, unroll=4)
        lines += [jnp.sum(a, 0, keepdims=True) for a in acc]
    if soft is not None:
        lines.append(soft[...])
    out[0] = jnp.concatenate(lines, 0).astype(bf16)
    for i in range(1, G):
        out[i] = out[0]


def row_total(ref, first, n):
    return jnp.sum(ref[:, first : first + n, :].astype(f32), 0)


def columns_kernel(masses, rowmass, columns, acc):
    r = 1.0 / (USERS * row_total(rowmass, 0, 2 * G))
    for v in range(2):
        scale = [jnp.broadcast_to(r[v * G + g : v * G + g + 1, :], (8, U)) for g in range(G)]

        def eight(s, _):
            at = pl.multiple_of(s * 8, 8)
            total = masses[0, v, pl.ds(at, 8), :] * scale[0]
            for g in range(1, G):
                total += masses[g, v, pl.ds(at, 8), :] * scale[g]
            acc[pl.ds(v * COLS + at, 8), :] = total[:, :128] + total[:, 128:]
            return 0

        lax.fori_loop(0, COLS // 8, eight, 0, unroll=4)
    send_columns(acc, columns)


def slopes_kernel(
    mine, other, proto, powered, masses, scale, first, last, keep, give, parts, acc, wide, ab, slopes
):
    acc[...] = jnp.zeros_like(acc)
    turned = jnp.concatenate([scale[...] * (1.0 / SHARP)] * 16, 0).T
    for i in range(2 * Q):
        wide[i * 128 : (i + 1) * 128, :] = jnp.broadcast_to(turned[:, i : i + 1], (128, 128))
    ab[0 : 2 * G, :] = (1.0 / SHARP) / row_total(first, 2 * G, 2 * G)
    ab[2 * G :, :] = 1.0 / row_total(last, 0, 2 * G)
    flat = proto[...].astype(f32).T.astype(bf16)
    own = lax.axis_index("x")

    def group(half, x, rows):
        g = place(half, x)
        far = x ^ own
        slot = (far >> 1) + 2 * (far & 1)
        for v in range(2):
            w = 1 - v
            a = ab[pl.ds(v * G + g, 1), :]
            b = ab[pl.ds(2 * G + w * G + g, 1), :]
            for q in range(Q):
                at = slice(q * 128, (q + 1) * 128)
                c = wide[(w * Q + q) * 128 : (w * Q + q + 1) * 128, :]
                slopes[v, at, :] = (
                    powered[g, v, at, :].astype(f32) * a
                    - masses[g, w, at, :] * jnp.concatenate([c, c], 1) * b
                ).astype(bf16)
            slope = slopes[v]
            made = jnp.dot(flat, slope, preferred_element_type=f32)
            (give if half else keep)[slot, v] = made.astype(bf16)
            acc[...] += jnp.dot(slope, rows[x, v], preferred_element_type=f32)

    groups(group, mine, other)
    parts[...] = acc[...].astype(bf16)


def finish_kernel(embeddings, inverse, kept, got, proto, grad_embed, grad_proto):
    for v in range(2):
        grad = (kept[v].astype(f32) + got[v].astype(f32)).T
        inv = inverse[v]
        unit = embeddings[v].astype(f32) * inv
        grad_embed[v] = inv * (grad - unit * jnp.sum(unit * grad, -1, keepdims=True))
    whole = proto[...].astype(f32).reshape(NY, G, 8, 128)
    whole = jnp.concatenate([whole[:, j].reshape(NY * 8, 128) for j in range(G)], 0)
    grad_proto[...] = whole.T


def swap(x, axis, n, bit):
    return lax.ppermute(x, axis, [(i, i ^ bit) for i in range(n)])


def plus(a, b):
    return (a.astype(f32) + b.astype(f32)).astype(bf16)


def body(embeddings, prototypes):
    kept = lambda dtype: shape((G, 2, COLS, U), dtype)
    sums = shape((NY * NZ * 8, 128), bf16)
    acc = pltpu.VMEM((2 * COLS, 128), f32)

    rows, inverse, proto = call(
        prepare_kernel,
        (shape((NX, 2, U, 128), bf16), shape((2, U, 1), f32), shape((NZ, SUB, 128), bf16)),
        embeddings,
        prototypes,
        scratch=[pltpu.VMEM((512, 128), f32)],
    )
    mine = lax.all_to_all(rows, "x", 0, 0)
    other = swap(mine, "c", NC, 1)
    proto = lax.all_to_all(proto, "z", 0, 0).reshape(COLS, 128)
    powered, masses, soft, columns = call(
        scores_kernel,
        (kept(bf16), kept(f32), shape((2 * G, U), f32), sums),
        mine,
        other,
        proto,
        scratch=[acc],
    )
    first = None
    for sweep in range(ITERS):
        columns = lax.all_to_all(columns, ("y", "z"), 0, 0, tiled=True)
        more = (soft,) if sweep == 0 else ()
        mass, scale = call(
            rows_kernel,
            (shape((G, 4 * G if more else 2 * G, U), bf16), shape((8, 128), f32)),
            masses,
            columns,
            *more,
            scratch=[acc],
        )
        mass = lax.all_to_all(mass, ("x", "c"), 0, 0)
        first = mass if first is None else first
        if sweep < ITERS - 1:
            columns = call(columns_kernel, sums, masses, mass, scratch=[acc])
    half = shape((NX, 2, 128, U), bf16)
    keep, give, parts = call(
        slopes_kernel,
        (half, half, shape((COLS, 128), bf16)),
        mine,
        other,
        proto,
        powered,
        masses,
        scale,
        first,
        mass,
        scratch=[
            pltpu.VMEM((COLS, 128), f32),
            acc,
            pltpu.VMEM((4 * G, U), f32),
            pltpu.VMEM((2, COLS, U), bf16),
        ],
    )
    unit = plus(keep, swap(give, "c", NC, 1))
    near = swap(unit[2:], "x", NX, 1)
    pieces = parts.reshape(NZ, NY, SUB // NY, 128).transpose(1, 0, 2, 3)
    pieces = pieces.reshape(NY * NZ, SUB // NY, 128)
    pieces = lax.all_to_all(pieces, ("y", "z"), 0, 0)
    unit = plus(unit[:2], near)
    far = swap(unit[1], "x", NX, 2)
    piece = jnp.sum(pieces.astype(f32), 0).astype(bf16)
    everyone = jnp.broadcast_to(piece[None], (NY * G, SUB // NY, 128))
    whole = lax.all_to_all(everyone, ("y", "x", "c"), 0, 0).reshape(COLS, 128)
    return tuple(
        call(
            finish_kernel,
            (shape((2, U, 128), f32), shape((128, COLS), f32)),
            embeddings,
            inverse,
            unit[0],
            far,
            whole,
        )
    )


def solution(mesh):
    fine = Mesh(mesh.devices.reshape(NY, NX, NC, NZ), ("y", "x", "c", "z"))
    placed = (P(None, ("y", "x", "c", "z"), None), P(None, "z"))
    return jax.shard_map(
        body, mesh=fine, in_specs=placed, out_specs=placed, check_vma=False
    )
```

```python
import functools

import jax
import jax.numpy as jnp
from jax import lax
from jax.experimental import pallas as pl
from jax.experimental.pallas import tpu as pltpu
from jax.sharding import Mesh, PartitionSpec as P

K = 4096
ITERS = 3
SINK = 0.05
SHARP = 0.1

NY, NX, NC, NZ = 8, 4, 2, 8
G = NX * NC
U = 256
SUB = 512 // G
COLS = NZ * SUB
Q = COLS // 128
USERS = NY * NX * NC * NZ * U
EPS = 1e-06
f32, bf16 = jnp.float32, jnp.bfloat16
VM = pl.BlockSpec(memory_space=pltpu.VMEM)
shape = jax.ShapeDtypeStruct


def call(kernel, outs, *args, scratch=(), flops=0):
    cost = pl.CostEstimate(flops=flops, bytes_accessed=1 << 20, transcendentals=0) if flops else None
    return pl.pallas_call(
        kernel,
        out_shape=outs,
        in_specs=[VM] * len(args),
        out_specs=jax.tree.map(lambda _: VM, outs),
        scratch_shapes=list(scratch),
        cost_estimate=cost,
        compiler_params=pltpu.CompilerParams(vmem_limit_bytes=20 * 1024 * 1024),
    )(*args)


def fold(x):
    return jnp.sum(x.reshape(-1, 8, x.shape[-1]), 0)


def users_kernel(embeddings, unit, inverse):
    for v in range(2):
        e = embeddings[v].astype(f32)
        inv = lax.rsqrt(jnp.sum(e * e, -1, keepdims=True) + EPS)
        inverse[v] = inv
        unit[v] = (e * inv).astype(bf16)


def proto_kernel(prototypes, proto, turned):
    turned[...] = prototypes[...].astype(f32).T
    j = lax.axis_index("x") * NC + lax.axis_index("c")
    own = turned[pl.ds(pl.multiple_of(j * SUB, SUB), SUB), :]
    own = (own * lax.rsqrt(jnp.sum(own * own, -1, keepdims=True) + EPS)).astype(bf16)
    for i in range(NZ):
        proto[i] = own


def send_columns(acc, out):
    rows = [jnp.sum(acc[i * 128 : (i + 1) * 128, :].T, 0, keepdims=True) for i in range(2 * Q)]
    part = jnp.concatenate(rows, 0)
    out[...] = jnp.concatenate([part] * (NY * NZ), 0).astype(out.dtype)


def groups(step, mine, other):
    for half, rows in enumerate((mine, other)):

        def member(r, _):
            step(half, r, rows)
            return 0

        lax.fori_loop(0, NX, member, 0)


def place(half, r):
    return lax.rem(lax.axis_index("c") + half, NC) * NX + (lax.axis_index("x") ^ r)


def scores_kernel(mine, other, proto, powered, masses, soft, columns, acc):
    acc[...] = jnp.zeros_like(acc)

    def group(half, x, rows):
        g = place(half, x)
        for v in range(2):
            rowsum = jnp.zeros((8, U), f32)
            for q in range(Q):
                at = slice(q * 128, (q + 1) * 128)
                s = lax.dot_general(
                    proto[at, :], rows[x, v], (((1,), (1,)), ((), ())), preferred_element_type=f32
                )
                e = jnp.exp(s * (1.0 / SHARP))
                k = e * e
                powered[g, v, at, :] = e.astype(bf16)
                masses[g, v, at, :] = k
                rowsum += fold(e)
                i = v * Q + q
                acc[i * 128 : (i + 1) * 128, :] += k[:, :128] + k[:, 128:]
            soft[pl.ds(v * G + g, 1), :] = jnp.sum(rowsum, 0, keepdims=True)

    groups(group, mine, other)
    send_columns(acc, columns)


def rows_kernel(sweep, masses, columns, *refs):
    soft = refs[0] if sweep == 0 else None
    out, wide = refs[-2 if sweep < ITERS - 1 else -3], refs[-1]
    c = 1.0 / (K * fold(columns[...].astype(f32)))
    if sweep == ITERS - 1:
        refs[-2][...] = c
    turned = jnp.concatenate([c] * 16, 0).T
    for i in range(2 * Q):
        wide[i * 128 : (i + 1) * 128, :] = jnp.broadcast_to(turned[:, i : i + 1], (128, 128))
    lines = []
    for v in range(2):

        def eight(s, acc):
            at = pl.multiple_of(s * 8, 8)
            cc = wide[pl.ds(v * COLS + at, 8), :]
            cc = jnp.concatenate([cc, cc], 1)
            return tuple(acc[g] + masses[g, v, pl.ds(at, 8), :] * cc for g in range(G))

        acc = lax.fori_loop(0, COLS // 8, eight, (jnp.zeros((8, U), f32),) * G, unroll=4)
        lines += [jnp.sum(a, 0, keepdims=True) for a in acc]
    if soft is not None:
        lines.append(soft[...])
    out[0] = jnp.concatenate(lines, 0).astype(bf16)
    for i in range(1, G):
        out[i] = out[0]


def row_total(ref, first, n):
    return jnp.sum(ref[:, first : first + n, :].astype(f32), 0)


def columns_kernel(masses, rowmass, columns, acc):
    r = 1.0 / (USERS * row_total(rowmass, 0, 2 * G))
    for v in range(2):
        scale = [jnp.broadcast_to(r[v * G + g : v * G + g + 1, :], (8, U)) for g in range(G)]

        def eight(s, _):
            at = pl.multiple_of(s * 8, 8)
            total = masses[0, v, pl.ds(at, 8), :] * scale[0]
            for g in range(1, G):
                total += masses[g, v, pl.ds(at, 8), :] * scale[g]
            acc[pl.ds(v * COLS + at, 8), :] = total[:, :128] + total[:, 128:]
            return 0

        lax.fori_loop(0, COLS // 8, eight, 0, unroll=4)
    send_columns(acc, columns)


def slopes_kernel(
    mine, other, powered, masses, scale, first, last, slopes, parts, acc, wide, ab
):
    acc[...] = jnp.zeros_like(acc)
    turned = jnp.concatenate([scale[...] * (1.0 / SHARP)] * 16, 0).T
    for i in range(2 * Q):
        wide[i * 128 : (i + 1) * 128, :] = jnp.broadcast_to(turned[:, i : i + 1], (128, 128))
    ab[0 : 2 * G, :] = (1.0 / SHARP) / row_total(first, 2 * G, 2 * G)
    ab[2 * G :, :] = 1.0 / row_total(last, 0, 2 * G)

    def group(half, r, rows):
        g = place(half, r)
        for v in range(2):
            w = 1 - v
            a = ab[pl.ds(v * G + g, 1), :]
            b = ab[pl.ds(2 * G + w * G + g, 1), :]
            for q in range(Q):
                at = slice(q * 128, (q + 1) * 128)
                c = wide[(w * Q + q) * 128 : (w * Q + q + 1) * 128, :]
                slopes[half * NX + r, v, at, :] = (
                    powered[g, v, at, :].astype(f32) * a
                    - masses[g, w, at, :] * jnp.concatenate([c, c], 1) * b
                ).astype(bf16)
            acc[...] += jnp.dot(slopes[half * NX + r, v], rows[r, v], preferred_element_type=f32)

    groups(group, mine, other)
    parts[...] = acc[...].astype(bf16)


def flat_kernel(proto, flat):
    flat[...] = proto[...].astype(f32).T.astype(bf16)


def units_kernel(flat, slopes, keep, give):

    def group(half, r, out):
        slot = lax.div(r, 2) + 2 * lax.rem(r, 2)
        for v in range(2):
            made = jnp.dot(flat[...], slopes[half * NX + r, v], preferred_element_type=f32)
            out[slot, v] = made.astype(bf16)

    groups(group, keep, give)


def piece_kernel(pieces, out):
    piece = fold(pieces[...].astype(f32))
    out[...] = jnp.concatenate([piece] * (NY * G), 0).astype(bf16)


def finish_kernel(embeddings, inverse, kept, got, proto, grad_embed, grad_proto):
    for v in range(2):
        grad = (kept[v].astype(f32) + got[v].astype(f32)).T
        inv = inverse[v]
        unit = embeddings[v].astype(f32) * inv
        grad_embed[v] = inv * (grad - unit * jnp.sum(unit * grad, -1, keepdims=True))
    whole = proto[...].astype(f32).reshape(NY, G, 8, 128)
    whole = jnp.concatenate([whole[:, j].reshape(NY * 8, 128) for j in range(G)], 0)
    grad_proto[...] = whole.T


def swap(x, axis, n, bit):
    return lax.ppermute(x, axis, [(i, i ^ bit) for i in range(n)])


def plus(a, b):
    return (a.astype(f32) + b.astype(f32)).astype(bf16)


def body(embeddings, prototypes):
    kept = lambda dtype: shape((G, 2, COLS, U), dtype)
    sums = shape((NY * NZ * 8, 128), bf16)
    acc = pltpu.VMEM((2 * COLS, 128), f32)

    proto = call(
        proto_kernel, shape((NZ, SUB, 128), bf16), prototypes, scratch=[pltpu.VMEM((512, 128), f32)]
    )
    proto = lax.all_to_all(proto, "z", 0, 0).reshape(COLS, 128)
    unit, inverse = call(
        users_kernel, (shape((2, U, 128), bf16), shape((2, U, 1), f32)), embeddings, flops=1 << 31
    )
    flat = call(flat_kernel, shape((128, COLS), bf16), proto, flops=1 << 36)
    others = [swap(unit, "x", NX, r) for r in (1, 2, 3)]
    others, flat = lax.optimization_barrier((others, flat))
    mine = jnp.stack([unit] + others)
    other = swap(mine, "c", NC, 1)
    powered, masses, soft, columns = call(
        scores_kernel,
        (kept(bf16), kept(f32), shape((2 * G, U), f32), sums),
        mine,
        other,
        proto,
        scratch=[acc],
    )
    first = None
    for sweep in range(ITERS):
        columns = lax.all_to_all(columns, ("y", "z"), 0, 0, tiled=True)
        lines = shape((G, 4 * G if sweep == 0 else 2 * G, U), bf16)
        mass = call(
            functools.partial(rows_kernel, sweep),
            (lines, shape((8, 128), f32)) if sweep == ITERS - 1 else lines,
            masses,
            columns,
            *((soft,) if sweep == 0 else ()),
            scratch=[acc],
        )
        if sweep == ITERS - 1:
            mass, scale = mass
        mass = lax.all_to_all(mass, ("x", "c"), 0, 0)
        first = mass if first is None else first
        if sweep < ITERS - 1:
            columns = call(columns_kernel, sums, masses, mass, scratch=[acc])
    slopes, parts = call(
        slopes_kernel,
        (kept(bf16), shape((COLS, 128), bf16)),
        mine,
        other,
        powered,
        masses,
        scale,
        first,
        mass,
        scratch=[pltpu.VMEM((COLS, 128), f32), acc, pltpu.VMEM((4 * G, U), f32)],
    )
    pieces = parts.reshape(NZ, NY, SUB // NY, 128).transpose(1, 0, 2, 3)
    pieces = lax.all_to_all(pieces.reshape(NY * NZ * 8, 128), ("y", "z"), 0, 0, tiled=True)
    half = shape((NX, 2, 128, U), bf16)
    keep, give = call(units_kernel, (half, half), flat, slopes, flops=1 << 31)
    unit = plus(keep, swap(give, "c", NC, 1))
    near = swap(unit[2:], "x", NX, 1)
    pieces = call(piece_kernel, shape((NY * G * 8, 128), bf16), pieces, flops=1 << 36)
    whole = lax.all_to_all(pieces, ("y", "x", "c"), 0, 0, tiled=True)
    unit = plus(unit[:2], near)
    far = swap(unit[1], "x", NX, 2)
    return tuple(
        call(
            finish_kernel,
            (shape((2, U, 128), f32), shape((128, COLS), f32)),
            embeddings,
            inverse,
            unit[0],
            far,
            whole,
        )
    )


def solution(mesh):
    fine = Mesh(mesh.devices.reshape(NY, NX, NC, NZ), ("y", "x", "c", "z"))
    placed = (P(None, ("y", "x", "c", "z"), None), P(None, "z"))
    return jax.shard_map(
        body, mesh=fine, in_specs=placed, out_specs=placed, check_vma=False
    )
```

```python
import functools

import jax
import jax.numpy as jnp
from jax import lax
from jax.experimental import pallas as pl
from jax.experimental.pallas import tpu as pltpu
from jax.sharding import Mesh, PartitionSpec as P

K = 4096
ITERS = 3
SINK = 0.05
SHARP = 0.1

NY, NX, NC, NZ = 8, 4, 2, 8
G = NX * NC
U = 256
SUB = 512 // G
COLS = NZ * SUB
Q = COLS // 128
USERS = NY * NX * NC * NZ * U
EPS = 1e-06
f32, bf16 = jnp.float32, jnp.bfloat16
VM = pl.BlockSpec(memory_space=pltpu.VMEM)
shape = jax.ShapeDtypeStruct


def call(kernel, outs, *args, scratch=(), flops=0):
    cost = pl.CostEstimate(flops=flops, bytes_accessed=1 << 20, transcendentals=0) if flops else None
    return pl.pallas_call(
        kernel,
        out_shape=outs,
        in_specs=[VM] * len(args),
        out_specs=jax.tree.map(lambda _: VM, outs),
        scratch_shapes=list(scratch),
        cost_estimate=cost,
        compiler_params=pltpu.CompilerParams(vmem_limit_bytes=20 * 1024 * 1024),
    )(*args)


def fold(x):
    return jnp.sum(x.reshape(-1, 8, x.shape[-1]), 0)


def prepare_kernel(embeddings, prototypes, rows, inverse, proto, users, columns, turned, sems):
    fetch = [
        pltpu.make_async_copy(src, dst, sems.at[i])
        for i, (src, dst) in enumerate(((embeddings, users), (prototypes, columns)))
    ]
    for copy in fetch:
        copy.start()
    fetch[0].wait()
    for v in range(2):
        e = users[v].astype(f32)
        inv = lax.rsqrt(jnp.sum(e * e, -1, keepdims=True) + EPS)
        inverse[v] = inv
        unit = (e * inv).astype(bf16)
        for i in range(NX):
            rows[i, v] = unit
    fetch[1].wait()
    turned[...] = columns[...].astype(f32).T
    j = lax.axis_index("x") * NC + lax.axis_index("c")
    own = turned[pl.ds(pl.multiple_of(j * SUB, SUB), SUB), :]
    own = (own * lax.rsqrt(jnp.sum(own * own, -1, keepdims=True) + EPS)).astype(bf16)
    for i in range(NZ):
        proto[i] = own


def send_columns(acc, out):
    rows = [jnp.sum(acc[i * 128 : (i + 1) * 128, :].T, 0, keepdims=True) for i in range(2 * Q)]
    part = jnp.concatenate(rows, 0)
    out[...] = jnp.concatenate([part] * (NY * NZ), 0).astype(out.dtype)


def groups(step, mine, other):
    for half, rows in enumerate((mine, other)):

        def member(x, _):
            step(half, x, rows)
            return 0

        lax.fori_loop(0, NX, member, 0)


def place(half, x):
    return lax.rem(lax.axis_index("c") + half, NC) * NX + x


def scores_kernel(mine, other, proto, powered, masses, soft, columns, acc):
    acc[...] = jnp.zeros_like(acc)

    def group(half, x, rows):
        g = place(half, x)
        for v in range(2):
            rowsum = jnp.zeros((8, U), f32)
            for q in range(Q):
                at = slice(q * 128, (q + 1) * 128)
                s = lax.dot_general(
                    proto[at, :], rows[x, v], (((1,), (1,)), ((), ())), preferred_element_type=f32
                )
                e = jnp.exp(s * (1.0 / SHARP))
                k = e * e
                powered[g, v, at, :] = e.astype(bf16)
                masses[g, v, at, :] = k
                rowsum += fold(e)
                i = v * Q + q
                acc[i * 128 : (i + 1) * 128, :] += k[:, :128] + k[:, 128:]
            soft[pl.ds(v * G + g, 1), :] = jnp.sum(rowsum, 0, keepdims=True)

    groups(group, mine, other)
    send_columns(acc, columns)


def rows_kernel(sweep, masses, columns, *refs):
    soft = refs[0] if sweep == 0 else None
    out, wide = refs[-2 if sweep < ITERS - 1 else -3], refs[-1]
    c = 1.0 / (K * fold(columns[...].astype(f32)))
    if sweep == ITERS - 1:
        refs[-2][...] = c
    turned = jnp.concatenate([c] * 16, 0).T
    for i in range(2 * Q):
        wide[i * 128 : (i + 1) * 128, :] = jnp.broadcast_to(turned[:, i : i + 1], (128, 128))
    lines = []
    for v in range(2):

        def eight(s, acc):
            at = pl.multiple_of(s * 8, 8)
            cc = wide[pl.ds(v * COLS + at, 8), :]
            cc = jnp.concatenate([cc, cc], 1)
            return tuple(acc[g] + masses[g, v, pl.ds(at, 8), :] * cc for g in range(G))

        acc = lax.fori_loop(0, COLS // 8, eight, (jnp.zeros((8, U), f32),) * G, unroll=4)
        lines += [jnp.sum(a, 0, keepdims=True) for a in acc]
    if soft is not None:
        lines.append(soft[...])
    out[0] = jnp.concatenate(lines, 0).astype(bf16)
    for i in range(1, G):
        out[i] = out[0]


def row_total(ref, first, n):
    return jnp.sum(ref[:, first : first + n, :].astype(f32), 0)


def columns_kernel(masses, rowmass, columns, acc):
    r = 1.0 / (USERS * row_total(rowmass, 0, 2 * G))
    for v in range(2):
        scale = [jnp.broadcast_to(r[v * G + g : v * G + g + 1, :], (8, U)) for g in range(G)]

        def eight(s, _):
            at = pl.multiple_of(s * 8, 8)
            total = masses[0, v, pl.ds(at, 8), :] * scale[0]
            for g in range(1, G):
                total += masses[g, v, pl.ds(at, 8), :] * scale[g]
            acc[pl.ds(v * COLS + at, 8), :] = total[:, :128] + total[:, 128:]
            return 0

        lax.fori_loop(0, COLS // 8, eight, 0, unroll=4)
    send_columns(acc, columns)


def flat_kernel(proto, flat):
    flat[...] = proto[...].astype(f32).T.astype(bf16)


def slopes_kernel(
    mine,
    other,
    flat,
    powered,
    masses,
    scale,
    first,
    last,
    keep,
    give0,
    give1,
    parts,
    acc,
    wide,
    ab,
    slopes,
):
    acc[...] = jnp.zeros_like(acc)
    turned = jnp.concatenate([scale[...] * (1.0 / SHARP)] * 16, 0).T
    for i in range(2 * Q):
        wide[i * 128 : (i + 1) * 128, :] = jnp.broadcast_to(turned[:, i : i + 1], (128, 128))
    ab[0 : 2 * G, :] = (1.0 / SHARP) / row_total(first, 2 * G, 2 * G)
    ab[2 * G :, :] = 1.0 / row_total(last, 0, 2 * G)

    def group(half, x, rows):
        g = place(half, x)
        far = x ^ lax.axis_index("x")
        slot = lax.div(far, 2) + 2 * lax.rem(far, 2)
        for v in range(2):
            w = 1 - v
            a = ab[pl.ds(v * G + g, 1), :]
            b = ab[pl.ds(2 * G + w * G + g, 1), :]
            for q in range(Q):
                at = slice(q * 128, (q + 1) * 128)
                c = wide[(w * Q + q) * 128 : (w * Q + q + 1) * 128, :]
                slopes[v, at, :] = (
                    powered[g, v, at, :].astype(f32) * a
                    - masses[g, w, at, :] * jnp.concatenate([c, c], 1) * b
                ).astype(bf16)
            made = jnp.dot(flat[...], slopes[v], preferred_element_type=f32)
            if half:
                (give0, give1)[v][slot] = made.astype(bf16)
            else:
                keep[v, slot] = made.astype(bf16)
            acc[...] += jnp.dot(slopes[v], rows[x, v], preferred_element_type=f32)

    groups(group, mine, other)
    for y in range(NY):
        for z in range(NZ):
            at = z * SUB + y * 8
            parts[(y * NZ + z) * 8 : (y * NZ + z + 1) * 8, :] = acc[at : at + 8, :]


def piece_kernel(pieces, out):
    out[...] = jnp.concatenate([fold(pieces[...])] * (NY * NX), 0).astype(bf16)


def cores_kernel(keep, got0, got1, stay, near):
    for v, got in enumerate((got0, got1)):
        for i in range(2):
            stay[v, i] = (keep[v, i].astype(f32) + got[i].astype(f32)).astype(bf16)
            near[v, i] = (keep[v, 2 + i].astype(f32) + got[2 + i].astype(f32)).astype(bf16)


def near_kernel(stay, got, unit, far):
    for v in range(2):
        unit[v] = stay[v, 0].astype(f32) + got[v, 0].astype(f32)
        far[v] = (stay[v, 1].astype(f32) + got[v, 1].astype(f32)).astype(bf16)


def finish_kernel(embeddings, inverse, kept, got, proto, grad_embed, grad_proto):
    for v in range(2):
        grad = (kept[v] + got[v].astype(f32)).T
        inv = inverse[v]
        unit = embeddings[v].astype(f32) * inv
        grad_embed[v] = inv * (grad - unit * jnp.sum(unit * grad, -1, keepdims=True))
    for x in range(NX):
        blocks = [proto[c].astype(f32).reshape(NY, NX, 8, 128)[:, x] for c in range(NC)]
        whole = jnp.concatenate([b.reshape(SUB, 128) for b in blocks], 0)
        grad_proto[:, x * NC * SUB : (x + 1) * NC * SUB] = whole.T


def swap(x, axis, n, bit):
    return lax.ppermute(x, axis, [(i, i ^ bit) for i in range(n)])


def body(embeddings, prototypes):
    kept = lambda dtype: shape((G, 2, COLS, U), dtype)
    sums = shape((NY * NZ * 8, 128), bf16)
    acc = pltpu.VMEM((2 * COLS, 128), f32)

    rows, inverse, proto = pl.pallas_call(
        prepare_kernel,
        out_shape=(
            shape((NX, 2, U, 128), bf16),
            shape((2, U, 1), f32),
            shape((NZ, SUB, 128), bf16),
        ),
        in_specs=[pl.BlockSpec(memory_space=pltpu.HBM)] * 2,
        out_specs=(VM,) * 3,
        scratch_shapes=[
            pltpu.VMEM((2, U, 128), bf16),
            pltpu.VMEM((128, 512), bf16),
            pltpu.VMEM((512, 128), f32),
            pltpu.SemaphoreType.DMA((2,)),
        ],
        compiler_params=pltpu.CompilerParams(vmem_limit_bytes=20 * 1024 * 1024),
    )(*(pltpu.with_memory_space_constraint(a, pltpu.HBM) for a in (embeddings, prototypes)))
    mine = lax.all_to_all(rows, "x", 0, 0)
    proto = lax.all_to_all(proto, "z", 0, 0).reshape(COLS, 128)
    other = swap(mine, "c", NC, 1)
    flat = call(flat_kernel, shape((128, COLS), bf16), proto, flops=1 << 36)
    proto, flat = lax.optimization_barrier((proto, flat))
    powered, masses, soft, columns = call(
        scores_kernel,
        (kept(bf16), kept(f32), shape((2 * G, U), f32), sums),
        mine,
        other,
        proto,
        scratch=[acc],
    )
    first = None
    for sweep in range(ITERS):
        columns = lax.all_to_all(columns, ("y", "z"), 0, 0, tiled=True)
        lines = shape((G, 4 * G if sweep == 0 else 2 * G, U), bf16)
        mass = call(
            functools.partial(rows_kernel, sweep),
            (lines, shape((8, 128), f32)) if sweep == ITERS - 1 else lines,
            masses,
            columns,
            *((soft,) if sweep == 0 else ()),
            scratch=[acc],
        )
        if sweep == ITERS - 1:
            mass, scale = mass
        mass = lax.all_to_all(mass, ("x", "c"), 0, 0)
        first = mass if first is None else first
        if sweep < ITERS - 1:
            columns = call(columns_kernel, sums, masses, mass, scratch=[acc])
    half, part = shape((2, NX, 128, U), bf16), shape((NX, 128, U), bf16)
    keep, give0, give1, parts = call(
        slopes_kernel,
        (half, part, part, shape((COLS, 128), f32)),
        mine,
        other,
        flat,
        powered,
        masses,
        scale,
        first,
        mass,
        scratch=[
            pltpu.VMEM((COLS, 128), f32),
            acc,
            pltpu.VMEM((4 * G, U), f32),
            pltpu.VMEM((2, COLS, U), bf16),
        ],
    )
    pieces = lax.all_to_all(parts, ("y", "z"), 0, 0, tiled=True)
    half = shape((2, 2, 128, U), bf16)
    stay, near = call(cores_kernel, (half, half), keep, *(swap(g, "c", NC, 1) for g in (give0, give1)))
    near = swap(near, "x", NX, 1)
    pieces = call(piece_kernel, shape((NY * NX * 8, 128), bf16), pieces, flops=1 << 36)
    whole = lax.all_to_all(pieces, ("y", "x"), 0, 0, tiled=True)
    whole = lax.all_gather(whole, "c", axis=0)
    unit, far = call(
        near_kernel, (shape((2, 128, U), f32), shape((2, 128, U), bf16)), stay, near
    )
    far = swap(far, "x", NX, 2)
    return tuple(
        call(
            finish_kernel,
            (shape((2, U, 128), f32), shape((128, COLS), f32)),
            embeddings,
            inverse,
            unit,
            far,
            whole,
        )
    )


def solution(mesh):
    fine = Mesh(mesh.devices.reshape(NY, NX, NC, NZ), ("y", "x", "c", "z"))
    placed = (P(None, ("y", "x", "c", "z"), None), P(None, "z"))
    return jax.shard_map(
        body, mesh=fine, in_specs=placed, out_specs=placed, check_vma=False
    )
```

```python
import functools

import jax
import jax.numpy as jnp
from jax import lax
from jax.experimental import pallas as pl
from jax.experimental.pallas import tpu as pltpu
from jax.sharding import Mesh, PartitionSpec as P

K = 4096
ITERS = 3
SINK = 0.05
SHARP = 0.1

NY, NX, NC, NZ = 8, 4, 2, 8
G = NX * NC
U = 256
SUB = 512 // G
COLS = NZ * SUB
Q = COLS // 128
USERS = NY * NX * NC * NZ * U
EPS = 1e-06
f32, bf16 = jnp.float32, jnp.bfloat16
VM = pl.BlockSpec(memory_space=pltpu.VMEM)
shape = jax.ShapeDtypeStruct


def call(kernel, outs, *args, scratch=(), flops=0):
    cost = pl.CostEstimate(flops=flops, bytes_accessed=1 << 20, transcendentals=0) if flops else None
    return pl.pallas_call(
        kernel,
        out_shape=outs,
        in_specs=[VM] * len(args),
        out_specs=jax.tree.map(lambda _: VM, outs),
        scratch_shapes=list(scratch),
        cost_estimate=cost,
        compiler_params=pltpu.CompilerParams(vmem_limit_bytes=20 * 1024 * 1024),
    )(*args)


def fold(x):
    return jnp.sum(x.reshape(-1, 8, x.shape[-1]), 0)


def prepare_kernel(
    embeddings, prototypes, rows, inverse, proto, users, columns, turned, copies, sems
):
    fetch = [
        pltpu.make_async_copy(src, dst, sems.at[i])
        for i, (src, dst) in enumerate(((prototypes, columns), (embeddings, users)))
    ]
    for copy in fetch:
        copy.start()
    fetch[0].wait()
    turned[...] = columns[...].astype(f32).T
    j = lax.axis_index("x") * NC + lax.axis_index("c")
    own = turned[pl.ds(pl.multiple_of(j * SUB, SUB), SUB), :]
    own = (own * lax.rsqrt(jnp.sum(own * own, -1, keepdims=True) + EPS)).astype(bf16)
    for i in range(NZ):
        copies[i] = own
    leave = pltpu.make_async_copy(copies, proto, sems.at[2])
    leave.start()
    fetch[1].wait()
    for v in range(2):
        e = users[v].astype(f32)
        inv = lax.rsqrt(jnp.sum(e * e, -1, keepdims=True) + EPS)
        inverse[v] = inv
        unit = (e * inv).astype(bf16)
        for i in range(NX):
            rows[i, v] = unit
    leave.wait()


def send_columns(acc, out):
    rows = [jnp.sum(acc[i * 128 : (i + 1) * 128, :].T, 0, keepdims=True) for i in range(2 * Q)]
    part = jnp.concatenate(rows, 0)
    out[...] = jnp.concatenate([part] * (NY * NZ), 0).astype(out.dtype)


def groups(step, mine, other):
    for half, rows in enumerate((mine, other)):

        def member(x, _):
            step(half, x, rows)
            return 0

        lax.fori_loop(0, NX, member, 0, unroll=True)


def place(half, x):
    return lax.rem(lax.axis_index("c") + half, NC) * NX + x


def scores_kernel(mine, other, proto, powered, masses, soft, columns, acc):
    acc[...] = jnp.zeros_like(acc)

    def group(half, x, rows):
        g = place(half, x)
        for v in range(2):
            rowsum = jnp.zeros((8, U), f32)
            for q in range(COLS // 256):
                at = slice(q * 256, (q + 1) * 256)
                s = lax.dot_general(
                    proto[at, :], rows[x, v], (((1,), (1,)), ((), ())), preferred_element_type=f32
                )
                e = jnp.exp(s * (1.0 / SHARP))
                k = e * e
                powered[g, v, at, :] = e.astype(bf16)
                masses[g, v, at, :] = k
                rowsum += fold(e)
                acc[v * COLS + q * 256 : v * COLS + (q + 1) * 256, :] += k[:, :128] + k[:, 128:]
            soft[pl.ds(v * G + g, 1), :] = jnp.sum(rowsum, 0, keepdims=True)

    groups(group, mine, other)
    send_columns(acc, columns)


def rows_kernel(sweep, masses, columns, *refs):
    soft = refs[0] if sweep == 0 else None
    out, wide = refs[-2 if sweep < ITERS - 1 else -3], refs[-1]
    c = 1.0 / (K * fold(columns[...].astype(f32)))
    if sweep == ITERS - 1:
        refs[-2][...] = c
    turned = jnp.concatenate([c] * 16, 0).T
    for i in range(2 * Q):
        wide[i * 128 : (i + 1) * 128, :] = jnp.broadcast_to(turned[:, i : i + 1], (128, 128))
    lines = []
    for v in range(2):

        def eight(s, acc):
            at = pl.multiple_of(s * 8, 8)
            cc = wide[pl.ds(v * COLS + at, 8), :]
            cc = jnp.concatenate([cc, cc], 1)
            return tuple(acc[g] + masses[g, v, pl.ds(at, 8), :] * cc for g in range(G))

        acc = lax.fori_loop(0, COLS // 8, eight, (jnp.zeros((8, U), f32),) * G, unroll=16)
        lines += [jnp.sum(a, 0, keepdims=True) for a in acc]
    if soft is not None:
        lines.append(soft[...])
    out[0] = jnp.concatenate(lines, 0).astype(bf16)
    for i in range(1, G):
        out[i] = out[0]


def row_total(ref, first, n):
    return jnp.sum(ref[:, first : first + n, :].astype(f32), 0)


def columns_kernel(masses, rowmass, columns, acc):
    r = 1.0 / (USERS * row_total(rowmass, 0, 2 * G))
    for v in range(2):
        scale = [jnp.broadcast_to(r[v * G + g : v * G + g + 1, :], (8, U)) for g in range(G)]

        def eight(s, _):
            at = pl.multiple_of(s * 8, 8)
            total = masses[0, v, pl.ds(at, 8), :] * scale[0]
            for g in range(1, G):
                total += masses[g, v, pl.ds(at, 8), :] * scale[g]
            acc[pl.ds(v * COLS + at, 8), :] = total[:, :128] + total[:, 128:]
            return 0

        lax.fori_loop(0, COLS // 8, eight, 0, unroll=16)
    send_columns(acc, columns)


def flat_kernel(proto, flat):
    flat[...] = proto[...].astype(f32).T.astype(bf16)


def slopes_kernel(
    mine,
    other,
    flat,
    powered,
    masses,
    scale,
    first,
    last,
    keep,
    give0,
    give1,
    parts,
    acc,
    wide,
    ab,
    slopes,
):
    acc[...] = jnp.zeros_like(acc)
    turned = jnp.concatenate([scale[...] * (1.0 / SHARP)] * 16, 0).T
    for i in range(2 * Q):
        wide[i * 128 : (i + 1) * 128, :] = jnp.broadcast_to(turned[:, i : i + 1], (128, 128))
    ab[0 : 2 * G, :] = (1.0 / SHARP) / row_total(first, 2 * G, 2 * G)
    ab[2 * G :, :] = 1.0 / row_total(last, 0, 2 * G)

    def group(half, x, rows):
        g = place(half, x)
        far = x ^ lax.axis_index("x")
        slot = lax.div(far, 2) + 2 * lax.rem(far, 2)
        slope = slopes.at[x % 2]
        for v in range(2):
            w = 1 - v
            a = ab[pl.ds(v * G + g, 1), :]
            b = ab[pl.ds(2 * G + w * G + g, 1), :]
            for q in range(Q):
                at = slice(q * 128, (q + 1) * 128)
                c = wide[(w * Q + q) * 128 : (w * Q + q + 1) * 128, :]
                slope[at, v * U : (v + 1) * U] = (
                    powered[g, v, at, :].astype(f32) * a
                    - masses[g, w, at, :] * jnp.concatenate([c, c], 1) * b
                ).astype(bf16)
        made = jnp.dot(flat[...], slope[...], preferred_element_type=f32).astype(bf16)
        for v in range(2):
            if half:
                (give0, give1)[v][slot] = made[:, v * U : (v + 1) * U]
            else:
                keep[v, slot] = made[:, v * U : (v + 1) * U]
        acc[...] += jnp.dot(slope[...], rows[x].reshape(2 * U, 128), preferred_element_type=f32)

    groups(group, mine, other)
    for y in range(NY):
        for z in range(NZ):
            at = z * SUB + y * 8
            parts[(y * NZ + z) * 8 : (y * NZ + z + 1) * 8, :] = acc[at : at + 8, :]


def piece_kernel(pieces, out):
    out[...] = jnp.concatenate([fold(pieces[...])] * (NY * NX), 0).astype(bf16)


def cores_kernel(keep, got0, got1, stay, near):
    for v, got in enumerate((got0, got1)):
        for i in range(2):
            stay[v, i] = (keep[v, i].astype(f32) + got[i].astype(f32)).astype(bf16)
            near[v, i] = (keep[v, 2 + i].astype(f32) + got[2 + i].astype(f32)).astype(bf16)


def near_kernel(stay, got, unit, far):
    for v in range(2):
        unit[v] = stay[v, 0].astype(f32) + got[v, 0].astype(f32)
        far[v] = (stay[v, 1].astype(f32) + got[v, 1].astype(f32)).astype(bf16)


def finish_kernel(embeddings, inverse, kept, got, proto, grad_embed, grad_proto):
    for v in range(2):
        grad = (kept[v] + got[v].astype(f32)).T
        inv = inverse[v]
        unit = embeddings[v].astype(f32) * inv
        grad_embed[v] = inv * (grad - unit * jnp.sum(unit * grad, -1, keepdims=True))
    for x in range(NX):
        blocks = [proto[c].astype(f32).reshape(NY, NX, 8, 128)[:, x] for c in range(NC)]
        whole = jnp.concatenate([b.reshape(SUB, 128) for b in blocks], 0)
        grad_proto[:, x * NC * SUB : (x + 1) * NC * SUB] = whole.T


def swap(x, axis, n, bit):
    return lax.ppermute(x, axis, [(i, i ^ bit) for i in range(n)])


def body(embeddings, prototypes):
    kept = lambda dtype: shape((G, 2, COLS, U), dtype)
    sums = shape((NY * NZ * 8, 128), bf16)
    acc = pltpu.VMEM((2 * COLS, 128), f32)

    rows, inverse, proto = pl.pallas_call(
        prepare_kernel,
        out_shape=(
            shape((NX, 2, U, 128), bf16),
            shape((2, U, 1), f32),
            shape((NZ, SUB, 128), bf16),
        ),
        in_specs=[pl.BlockSpec(memory_space=pltpu.HBM)] * 2,
        out_specs=(VM, VM, pl.BlockSpec(memory_space=pl.ANY)),
        scratch_shapes=[
            pltpu.VMEM((2, U, 128), bf16),
            pltpu.VMEM((128, 512), bf16),
            pltpu.VMEM((512, 128), f32),
            pltpu.VMEM((NZ, SUB, 128), bf16),
            pltpu.SemaphoreType.DMA((3,)),
        ],
        compiler_params=pltpu.CompilerParams(vmem_limit_bytes=20 * 1024 * 1024),
    )(*(pltpu.with_memory_space_constraint(a, pltpu.HBM) for a in (embeddings, prototypes)))
    mine = lax.all_to_all(rows, "x", 0, 0)
    proto = lax.all_to_all(proto, "z", 0, 0).reshape(COLS, 128)
    other = swap(mine, "c", NC, 1)
    flat = call(flat_kernel, shape((128, COLS), bf16), proto, flops=1 << 36)
    proto, flat = lax.optimization_barrier((proto, flat))
    powered, masses, soft, columns = call(
        scores_kernel,
        (kept(bf16), kept(f32), shape((2 * G, U), f32), sums),
        mine,
        other,
        proto,
        scratch=[acc],
    )
    first = None
    for sweep in range(ITERS):
        columns = lax.all_to_all(columns, ("y", "z"), 0, 0, tiled=True)
        lines = shape((G, 4 * G if sweep == 0 else 2 * G, U), bf16)
        mass = call(
            functools.partial(rows_kernel, sweep),
            (lines, shape((8, 128), f32)) if sweep == ITERS - 1 else lines,
            masses,
            columns,
            *((soft,) if sweep == 0 else ()),
            scratch=[acc],
        )
        if sweep == ITERS - 1:
            mass, scale = mass
        mass = lax.all_to_all(mass, ("x", "c"), 0, 0)
        first = mass if first is None else first
        if sweep < ITERS - 1:
            columns = call(columns_kernel, sums, masses, mass, scratch=[acc])
    half, part = shape((2, NX, 128, U), bf16), shape((NX, 128, U), bf16)
    keep, give0, give1, parts = call(
        slopes_kernel,
        (half, part, part, shape((COLS, 128), f32)),
        mine,
        other,
        flat,
        powered,
        masses,
        scale,
        first,
        mass,
        scratch=[
            pltpu.VMEM((COLS, 128), f32),
            acc,
            pltpu.VMEM((4 * G, U), f32),
            pltpu.VMEM((2, COLS, 2 * U), bf16),
        ],
    )
    pieces = lax.all_to_all(parts, ("y", "z"), 0, 0, tiled=True)
    half = shape((2, 2, 128, U), bf16)
    stay, near = call(cores_kernel, (half, half), keep, *(swap(g, "c", NC, 1) for g in (give0, give1)))
    near = swap(near, "x", NX, 1)
    pieces = call(piece_kernel, shape((NY * NX * 8, 128), bf16), pieces, flops=1 << 36)
    whole = lax.all_to_all(pieces, ("y", "x"), 0, 0, tiled=True)
    whole = lax.all_gather(whole, "c", axis=0)
    unit, far = call(
        near_kernel, (shape((2, 128, U), f32), shape((2, 128, U), bf16)), stay, near
    )
    far = swap(far, "x", NX, 2)
    return tuple(
        call(
            finish_kernel,
            (shape((2, U, 128), f32), shape((128, COLS), f32)),
            embeddings,
            inverse,
            unit,
            far,
            whole,
        )
    )


def solution(mesh):
    fine = Mesh(mesh.devices.reshape(NY, NX, NC, NZ), ("y", "x", "c", "z"))
    placed = (P(None, ("y", "x", "c", "z"), None), P(None, "z"))
    return jax.shard_map(
        body, mesh=fine, in_specs=placed, out_specs=placed, check_vma=False
    )
```

```python
import functools

import jax
import jax.numpy as jnp
from jax import lax
from jax.experimental import pallas as pl
from jax.experimental.pallas import tpu as pltpu
from jax.sharding import Mesh, PartitionSpec as P

K = 4096
ITERS = 3
SINK = 0.05
SHARP = 0.1

NY, NX, NC, NZ = 8, 4, 2, 8
G = NX * NC
U = 256
SUB = 512 // G
COLS = NZ * SUB
Q = COLS // 128
USERS = NY * NX * NC * NZ * U
EPS = 1e-06
f32, bf16 = jnp.float32, jnp.bfloat16
VM = pl.BlockSpec(memory_space=pltpu.VMEM)
shape = jax.ShapeDtypeStruct


def call(kernel, outs, *args, scratch=(), flops=0, aliases={}):
    cost = pl.CostEstimate(flops=flops, bytes_accessed=1 << 20, transcendentals=0) if flops else None
    return pl.pallas_call(
        kernel,
        out_shape=outs,
        in_specs=[VM] * len(args),
        out_specs=jax.tree.map(lambda _: VM, outs),
        scratch_shapes=list(scratch),
        cost_estimate=cost,
        input_output_aliases=aliases,
        compiler_params=pltpu.CompilerParams(vmem_limit_bytes=20 * 1024 * 1024),
    )(*args)


def fold(x):
    return jnp.sum(x.reshape(-1, 8, x.shape[-1]), 0)


def prepare_kernel(
    embeddings, prototypes, unit, inverse, proto, users, columns, turned, copies, sems
):
    fetch = [
        pltpu.make_async_copy(src, dst, sems.at[i])
        for i, (src, dst) in enumerate(((prototypes, columns), (embeddings, users)))
    ]
    for copy in fetch:
        copy.start()
    fetch[0].wait()
    turned[...] = columns[...].astype(f32).T
    j = lax.axis_index("x") * NC + lax.axis_index("c")
    own = turned[pl.ds(pl.multiple_of(j * SUB, SUB), SUB), :]
    own = (own * lax.rsqrt(jnp.sum(own * own, -1, keepdims=True) + EPS)).astype(bf16)
    for i in range(NZ):
        copies[i] = own
    leave = pltpu.make_async_copy(copies, proto, sems.at[2])
    leave.start()
    fetch[1].wait()
    for v in range(2):
        e = users[v].astype(f32)
        inv = lax.rsqrt(jnp.sum(e * e, -1, keepdims=True) + EPS)
        inverse[v] = inv
        unit[v] = (e * inv).astype(bf16)
    leave.wait()


def send_columns(acc, out):
    rows = [jnp.sum(acc[i * 128 : (i + 1) * 128, :].T, 0, keepdims=True) for i in range(2 * Q)]
    part = jnp.concatenate(rows, 0)
    out[...] = jnp.concatenate([part] * (NY * NZ), 0).astype(out.dtype)


def members(step):
    def member(r, _):
        step(r)
        return 0

    lax.fori_loop(0, NX, member, 0, unroll=True)


def place(half, r):
    return lax.rem(lax.axis_index("c") + half, NC) * NX + (lax.axis_index("x") ^ r)


def scores_kernel(half, rows, proto, *refs):
    powered, masses, soft, acc = refs if half == 0 else refs[4:8]
    if half == 0:
        acc[...] = jnp.zeros_like(acc)

    def group(r):
        g = place(half, r)
        for v in range(2):
            rowsum = jnp.zeros((8, U), f32)
            for q in range(COLS // 256):
                at = slice(q * 256, (q + 1) * 256)
                s = lax.dot_general(
                    proto[at, :], rows[r, v], (((1,), (1,)), ((), ())), preferred_element_type=f32
                )
                e = jnp.exp(s * (1.0 / SHARP))
                k = e * e
                powered[g, v, at, :] = e.astype(bf16)
                masses[g, v, at, :] = k
                rowsum += fold(e)
                acc[v * COLS + q * 256 : v * COLS + (q + 1) * 256, :] += k[:, :128] + k[:, 128:]
            soft[pl.ds(v * G + g, 1), :] = jnp.sum(rowsum, 0, keepdims=True)

    members(group)
    if half:
        send_columns(acc, refs[-1])


def rows_kernel(sweep, masses, columns, *refs):
    soft = refs[0] if sweep == 0 else None
    out, wide = refs[-2 if sweep < ITERS - 1 else -3], refs[-1]
    c = 1.0 / (K * fold(columns[...].astype(f32)))
    if sweep == ITERS - 1:
        refs[-2][...] = c
    turned = jnp.concatenate([c] * 16, 0).T
    for i in range(2 * Q):
        wide[i * 128 : (i + 1) * 128, :] = jnp.broadcast_to(turned[:, i : i + 1], (128, 128))
    lines = []
    for v in range(2):

        def eight(s, acc):
            at = pl.multiple_of(s * 8, 8)
            cc = wide[pl.ds(v * COLS + at, 8), :]
            cc = jnp.concatenate([cc, cc], 1)
            return tuple(acc[g] + masses[g, v, pl.ds(at, 8), :] * cc for g in range(G))

        acc = lax.fori_loop(0, COLS // 8, eight, (jnp.zeros((8, U), f32),) * G, unroll=16)
        lines += [jnp.sum(a, 0, keepdims=True) for a in acc]
    if soft is not None:
        lines.append(soft[...])
    out[0] = jnp.concatenate(lines, 0).astype(bf16)
    for i in range(1, G):
        out[i] = out[0]


def row_total(ref, first, n):
    return jnp.sum(ref[:, first : first + n, :].astype(f32), 0)


def columns_kernel(masses, rowmass, columns, acc):
    r = 1.0 / (USERS * row_total(rowmass, 0, 2 * G))
    for v in range(2):
        scale = [jnp.broadcast_to(r[v * G + g : v * G + g + 1, :], (8, U)) for g in range(G)]

        def eight(s, _):
            at = pl.multiple_of(s * 8, 8)
            total = masses[0, v, pl.ds(at, 8), :] * scale[0]
            for g in range(1, G):
                total += masses[g, v, pl.ds(at, 8), :] * scale[g]
            acc[pl.ds(v * COLS + at, 8), :] = total[:, :128] + total[:, 128:]
            return 0

        lax.fori_loop(0, COLS // 8, eight, 0, unroll=16)
    send_columns(acc, columns)


def flat_kernel(proto, flat):
    flat[...] = proto[...].astype(f32).T.astype(bf16)


def slopes_kernel(
    mine,
    other,
    flat,
    powered,
    masses,
    scale,
    first,
    last,
    keep,
    give0,
    give1,
    parts,
    acc,
    wide,
    ab,
    slopes,
):
    acc[...] = jnp.zeros_like(acc)
    turned = jnp.concatenate([scale[...] * (1.0 / SHARP)] * 16, 0).T
    for i in range(2 * Q):
        wide[i * 128 : (i + 1) * 128, :] = jnp.broadcast_to(turned[:, i : i + 1], (128, 128))
    ab[0 : 2 * G, :] = (1.0 / SHARP) / row_total(first, 2 * G, 2 * G)
    ab[2 * G :, :] = 1.0 / row_total(last, 0, 2 * G)

    def group(half, r, rows):
        g = place(half, r)
        slot = ((r << 1) & 3) ^ ((r >> 1) * 3)
        slope = slopes.at[r % 2]
        for v in range(2):
            w = 1 - v
            a = ab[pl.ds(v * G + g, 1), :]
            b = ab[pl.ds(2 * G + w * G + g, 1), :]
            for q in range(Q):
                at = slice(q * 128, (q + 1) * 128)
                c = wide[(w * Q + q) * 128 : (w * Q + q + 1) * 128, :]
                slope[at, v * U : (v + 1) * U] = (
                    powered[g, v, at, :].astype(f32) * a
                    - masses[g, w, at, :] * jnp.concatenate([c, c], 1) * b
                ).astype(bf16)
        made = jnp.dot(flat[...], slope[...], preferred_element_type=f32).astype(bf16)
        for v in range(2):
            if half:
                (give0, give1)[v][slot] = made[:, v * U : (v + 1) * U]
            else:
                keep[v, slot] = made[:, v * U : (v + 1) * U]
        acc[...] += jnp.dot(slope[...], rows[r].reshape(2 * U, 128), preferred_element_type=f32)

    for half, rows in enumerate((mine, other)):
        members(lambda r, half=half, rows=rows: group(half, r, rows))
    for y in range(NY):
        for z in range(NZ):
            at = z * SUB + y * 8
            parts[(y * NZ + z) * 8 : (y * NZ + z + 1) * 8, :] = acc[at : at + 8, :]


def piece_kernel(pieces, out):
    out[...] = jnp.concatenate([fold(pieces[...])] * (NY * NX), 0).astype(bf16)


def cores_kernel(keep, got0, got1, stay, near):
    for v, got in enumerate((got0, got1)):
        for i in range(2):
            stay[v, i] = (keep[v, i].astype(f32) + got[i].astype(f32)).astype(bf16)
            near[v, i] = (keep[v, 2 + i].astype(f32) + got[2 + i].astype(f32)).astype(bf16)


def near_kernel(stay, got, unit, far):
    for v in range(2):
        unit[v] = stay[v, 0].astype(f32) + got[v, 0].astype(f32)
        far[v] = (stay[v, 1].astype(f32) + got[v, 1].astype(f32)).astype(bf16)


def finish_kernel(embeddings, inverse, kept, got, proto, grad_embed, grad_proto):
    for v in range(2):
        grad = (kept[v] + got[v].astype(f32)).T
        inv = inverse[v]
        unit = embeddings[v].astype(f32) * inv
        grad_embed[v] = inv * (grad - unit * jnp.sum(unit * grad, -1, keepdims=True))
    for x in range(NX):
        blocks = [proto[c].astype(f32).reshape(NY, NX, 8, 128)[:, x] for c in range(NC)]
        whole = jnp.concatenate([b.reshape(SUB, 128) for b in blocks], 0)
        grad_proto[:, x * NC * SUB : (x + 1) * NC * SUB] = whole.T


def swap(x, axis, n, bit):
    return lax.ppermute(x, axis, [(i, i ^ bit) for i in range(n)])


def body(embeddings, prototypes):
    kept = lambda dtype: shape((G, 2, COLS, U), dtype)
    sums = shape((NY * NZ * 8, 128), bf16)
    acc = pltpu.VMEM((2 * COLS, 128), f32)

    unit, inverse, proto = pl.pallas_call(
        prepare_kernel,
        out_shape=(
            shape((2, U, 128), bf16),
            shape((2, U, 1), f32),
            shape((NZ, SUB, 128), bf16),
        ),
        in_specs=[pl.BlockSpec(memory_space=pltpu.HBM)] * 2,
        out_specs=(VM, VM, pl.BlockSpec(memory_space=pl.ANY)),
        scratch_shapes=[
            pltpu.VMEM((2, U, 128), bf16),
            pltpu.VMEM((128, 512), bf16),
            pltpu.VMEM((512, 128), f32),
            pltpu.VMEM((NZ, SUB, 128), bf16),
            pltpu.SemaphoreType.DMA((3,)),
        ],
        compiler_params=pltpu.CompilerParams(vmem_limit_bytes=20 * 1024 * 1024),
    )(*(pltpu.with_memory_space_constraint(a, pltpu.HBM) for a in (embeddings, prototypes)))
    proto = lax.all_to_all(proto, "z", 0, 0).reshape(COLS, 128)
    others = [swap(unit, "x", NX, r) for r in range(1, NX)]
    flat = call(flat_kernel, shape((128, COLS), bf16), proto, flops=1 << 36)
    others, proto, flat = lax.optimization_barrier((others, proto, flat))
    mine = jnp.stack([unit] + others)
    other = swap(mine, "c", NC, 1)
    part = shape((2 * COLS, 128), f32)
    grid = (kept(bf16), kept(f32), shape((2 * G, U), f32))
    half = call(
        functools.partial(scores_kernel, 0),
        (*grid, part),
        mine,
        proto,
        flops=1 << 31,
    )
    powered, masses, soft, _, columns = call(
        functools.partial(scores_kernel, 1),
        (*grid, part, sums),
        other,
        proto,
        *half,
        aliases={2: 0, 3: 1, 4: 2, 5: 3},
    )
    first = None
    for sweep in range(ITERS):
        columns = lax.all_to_all(columns, ("y", "z"), 0, 0, tiled=True)
        lines = shape((G, 4 * G if sweep == 0 else 2 * G, U), bf16)
        mass = call(
            functools.partial(rows_kernel, sweep),
            (lines, shape((8, 128), f32)) if sweep == ITERS - 1 else lines,
            masses,
            columns,
            *((soft,) if sweep == 0 else ()),
            scratch=[acc],
        )
        if sweep == ITERS - 1:
            mass, scale = mass
        mass = lax.all_to_all(mass, ("x", "c"), 0, 0)
        first = mass if first is None else first
        if sweep < ITERS - 1:
            columns = call(columns_kernel, sums, masses, mass, scratch=[acc])
    half, part = shape((2, NX, 128, U), bf16), shape((NX, 128, U), bf16)
    keep, give0, give1, parts = call(
        slopes_kernel,
        (half, part, part, shape((COLS, 128), f32)),
        mine,
        other,
        flat,
        powered,
        masses,
        scale,
        first,
        mass,
        scratch=[
            pltpu.VMEM((COLS, 128), f32),
            acc,
            pltpu.VMEM((4 * G, U), f32),
            pltpu.VMEM((2, COLS, 2 * U), bf16),
        ],
    )
    pieces = lax.all_to_all(parts, ("y", "z"), 0, 0, tiled=True)
    half = shape((2, 2, 128, U), bf16)
    stay, near = call(cores_kernel, (half, half), keep, *(swap(g, "c", NC, 1) for g in (give0, give1)))
    near = swap(near, "x", NX, 1)
    pieces = call(piece_kernel, shape((NY * NX * 8, 128), bf16), pieces, flops=1 << 36)
    whole = lax.all_to_all(pieces, ("y", "x"), 0, 0, tiled=True)
    whole = lax.all_gather(whole, "c", axis=0)
    unit, far = call(
        near_kernel, (shape((2, 128, U), f32), shape((2, 128, U), bf16)), stay, near
    )
    far = swap(far, "x", NX, 3)
    return tuple(
        call(
            finish_kernel,
            (shape((2, U, 128), f32), shape((128, COLS), f32)),
            embeddings,
            inverse,
            unit,
            far,
            whole,
        )
    )


def solution(mesh):
    fine = Mesh(mesh.devices.reshape(NY, NX, NC, NZ), ("y", "x", "c", "z"))
    placed = (P(None, ("y", "x", "c", "z"), None), P(None, "z"))
    return jax.shard_map(
        body, mesh=fine, in_specs=placed, out_specs=placed, check_vma=False
    )
```

```python
import functools

import jax
import jax.numpy as jnp
from jax import lax
from jax.experimental import pallas as pl
from jax.experimental.pallas import tpu as pltpu
from jax.sharding import Mesh, PartitionSpec as P

K = 4096
ITERS = 3
SINK = 0.05
SHARP = 0.1

NY, NX, NC, NZ = 8, 4, 2, 8
G = NX * NC
U = 256
SUB = 512 // G
COLS = NZ * SUB
Q = COLS // 128
USERS = NY * NX * NC * NZ * U
EPS = 1e-06
f32, bf16 = jnp.float32, jnp.bfloat16
VM = pl.BlockSpec(memory_space=pltpu.VMEM)
shape = jax.ShapeDtypeStruct


SIZES = dict(y=NY, x=NX, c=NC, z=NZ)
FIRST = dict(y=4, x=2, c=0, z=4)


def order(axes):
    places = [[]]
    for a in axes:
        places = [p + [(i + FIRST[a]) % SIZES[a]] for p in places for i in range(SIZES[a])]
    return places


def exchange(x, axes):
    members = []
    for place_ in order(axes):
        at = 0
        for a, i in zip(axes, place_):
            at = at * SIZES[a] + i
        members.append(at)
    axis = axes if len(axes) > 1 else axes[0]
    return lax.all_to_all(x, axis, 0, 0, tiled=True, axis_index_groups=[members])


def call(kernel, outs, *args, scratch=(), flops=0):
    cost = pl.CostEstimate(flops=flops, bytes_accessed=1 << 20, transcendentals=0) if flops else None
    return pl.pallas_call(
        kernel,
        out_shape=outs,
        in_specs=[VM] * len(args),
        out_specs=jax.tree.map(lambda _: VM, outs),
        scratch_shapes=list(scratch),
        cost_estimate=cost,
        compiler_params=pltpu.CompilerParams(vmem_limit_bytes=20 * 1024 * 1024),
    )(*args)


def fold(x):
    return jnp.sum(x.reshape(-1, 8, x.shape[-1]), 0)


def prepare_kernel(
    embeddings, prototypes, rows, inverse, proto, users, columns, turned, copies, sems
):
    fetch = [
        pltpu.make_async_copy(src, dst, sems.at[i])
        for i, (src, dst) in enumerate(((prototypes, columns), (embeddings, users)))
    ]
    for copy in fetch:
        copy.start()
    fetch[0].wait()
    turned[...] = columns[...].astype(f32).T
    j = lax.axis_index("x") * NC + lax.axis_index("c")
    own = turned[pl.ds(pl.multiple_of(j * SUB, SUB), SUB), :]
    own = (own * lax.rsqrt(jnp.sum(own * own, -1, keepdims=True) + EPS)).astype(bf16)
    for i in range(NZ):
        copies[i] = own
    leave = pltpu.make_async_copy(copies, proto, sems.at[2])
    leave.start()
    fetch[1].wait()
    for v in range(2):
        e = users[v].astype(f32)
        inv = lax.rsqrt(jnp.sum(e * e, -1, keepdims=True) + EPS)
        inverse[v] = inv
        unit = (e * inv).astype(bf16)
        for i in range(NX):
            rows[i, v] = unit
    leave.wait()


def send_columns(acc, out):
    rows = [jnp.sum(acc[i * 128 : (i + 1) * 128, :].T, 0, keepdims=True) for i in range(2 * Q)]
    part = jnp.concatenate(rows, 0)
    out[...] = jnp.concatenate([part] * (NY * NZ), 0).astype(out.dtype)


def groups(step, mine, other):
    for half, rows in enumerate((mine, other)):

        def member(x, _):
            step(half, x, rows)
            return 0

        lax.fori_loop(0, NX, member, 0, unroll=True)


def place(half, x):
    return lax.rem(lax.axis_index("c") + half, NC) * NX + x


def scores_kernel(mine, other, proto, powered, masses, soft, columns, acc):
    acc[...] = jnp.zeros_like(acc)

    def group(half, x, rows):
        g = place(half, x)
        for v in range(2):
            rowsum = jnp.zeros((8, U), f32)
            for q in range(COLS // 256):
                at = slice(q * 256, (q + 1) * 256)
                s = lax.dot_general(
                    proto[at, :], rows[x, v], (((1,), (1,)), ((), ())), preferred_element_type=f32
                )
                e = jnp.exp(s * (1.0 / SHARP))
                k = e * e
                powered[g, v, at, :] = e.astype(bf16)
                masses[g, v, at, :] = k
                rowsum += fold(e)
                acc[v * COLS + q * 256 : v * COLS + (q + 1) * 256, :] += k[:, :128] + k[:, 128:]
            soft[pl.ds(v * G + g, 1), :] = jnp.sum(rowsum, 0, keepdims=True)

    groups(group, mine, other)
    send_columns(acc, columns)


def rows_kernel(sweep, masses, columns, *refs):
    soft = refs[0] if sweep == 0 else None
    out, wide = refs[-2 if sweep < ITERS - 1 else -3], refs[-1]
    c = 1.0 / (K * fold(columns[...].astype(f32)))
    if sweep == ITERS - 1:
        refs[-2][...] = c
    turned = jnp.concatenate([c] * 16, 0).T
    for i in range(2 * Q):
        wide[i * 128 : (i + 1) * 128, :] = jnp.broadcast_to(turned[:, i : i + 1], (128, 128))
    lines = []
    for v in range(2):

        def eight(s, acc):
            at = pl.multiple_of(s * 8, 8)
            cc = wide[pl.ds(v * COLS + at, 8), :]
            cc = jnp.concatenate([cc, cc], 1)
            return tuple(acc[g] + masses[g, v, pl.ds(at, 8), :] * cc for g in range(G))

        acc = lax.fori_loop(0, COLS // 8, eight, (jnp.zeros((8, U), f32),) * G, unroll=16)
        lines += [jnp.sum(a, 0, keepdims=True) for a in acc]
    if soft is not None:
        lines.append(soft[...])
    out[0] = jnp.concatenate(lines, 0).astype(bf16)
    for i in range(1, G):
        out[i] = out[0]


def row_total(ref, first, n):
    return jnp.sum(ref[:, first : first + n, :].astype(f32), 0)


def columns_kernel(masses, rowmass, columns, acc):
    r = 1.0 / (USERS * row_total(rowmass, 0, 2 * G))
    for v in range(2):
        scale = [jnp.broadcast_to(r[v * G + g : v * G + g + 1, :], (8, U)) for g in range(G)]

        def eight(s, _):
            at = pl.multiple_of(s * 8, 8)
            total = masses[0, v, pl.ds(at, 8), :] * scale[0]
            for g in range(1, G):
                total += masses[g, v, pl.ds(at, 8), :] * scale[g]
            acc[pl.ds(v * COLS + at, 8), :] = total[:, :128] + total[:, 128:]
            return 0

        lax.fori_loop(0, COLS // 8, eight, 0, unroll=16)
    send_columns(acc, columns)


def flat_kernel(proto, flat):
    flat[...] = proto[...].astype(f32).T.astype(bf16)


def slopes_kernel(
    mine,
    other,
    flat,
    powered,
    masses,
    scale,
    first,
    last,
    stay,
    near,
    give_stay,
    give_near,
    parts,
    acc,
    wide,
    ab,
    slopes,
    units,
):
    acc[...] = jnp.zeros_like(acc)
    turned = jnp.concatenate([scale[...] * (1.0 / SHARP)] * 16, 0).T
    for i in range(2 * Q):
        wide[i * 128 : (i + 1) * 128, :] = jnp.broadcast_to(turned[:, i : i + 1], (128, 128))
    ab[0 : 2 * G, :] = (1.0 / SHARP) / row_total(first, 2 * G, 2 * G)
    ab[2 * G :, :] = 1.0 / row_total(last, 0, 2 * G)

    def group(half, x, rows):
        g = place(half, x)
        far = lax.rem(x + FIRST["x"], NX) ^ lax.axis_index("x")
        slot = ((far << 1) & 3) ^ ((far >> 1) * 3)
        slope = slopes.at[x % 2]
        for v in range(2):
            w = 1 - v
            a = ab[pl.ds(v * G + g, 1), :]
            b = ab[pl.ds(2 * G + w * G + g, 1), :]
            for q in range(Q):
                at = slice(q * 128, (q + 1) * 128)
                c = wide[(w * Q + q) * 128 : (w * Q + q + 1) * 128, :]
                slope[at, v * U : (v + 1) * U] = (
                    powered[g, v, at, :].astype(f32) * a
                    - masses[g, w, at, :] * jnp.concatenate([c, c], 1) * b
                ).astype(bf16)
        made = jnp.dot(flat[...], slope[...], preferred_element_type=f32).astype(bf16)
        for v in range(2):
            units[half, slot, v] = made[:, v * U : (v + 1) * U]
        acc[...] += jnp.dot(slope[...], rows[x].reshape(2 * U, 128), preferred_element_type=f32)

    groups(group, mine, other)
    for i in range(2):
        for v in range(2):
            stay[v, i], near[v, i] = units[0, i, v], units[0, 2 + i, v]
            give_stay[v, i], give_near[v, i] = units[1, i, v], units[1, 2 + i, v]
    for i, (y, z) in enumerate(order(("y", "z"))):
        at = (z - FIRST["z"]) % NZ * SUB + y * 8
        parts[i * 8 : (i + 1) * 8, :] = acc[at : at + 8, :]


def piece_kernel(pieces, out):
    out[...] = jnp.concatenate([fold(pieces[...])] * (NY * NX), 0).astype(bf16)


def add_kernel(mine, got, out):
    out[...] = (mine[...].astype(f32) + got[...].astype(f32)).astype(bf16)


def near_kernel(stay, other, got, unit, far):
    for v in range(2):
        unit[v] = stay[v, 0].astype(f32) + other[v, 0].astype(f32) + got[v, 0].astype(f32)
        last = stay[v, 1].astype(f32) + other[v, 1].astype(f32) + got[v, 1].astype(f32)
        far[v] = last.astype(bf16)


def finish_kernel(embeddings, inverse, kept, got, proto, grad_embed, grad_proto):
    for v in range(2):
        grad = (kept[v] + got[v].astype(f32)).T
        inv = inverse[v]
        unit = embeddings[v].astype(f32) * inv
        grad_embed[v] = inv * (grad - unit * jnp.sum(unit * grad, -1, keepdims=True))
    for x in range(NX):
        blocks = []
        for c in range(NC):
            b = proto[c].astype(f32).reshape(NY, NX, 8, 128)[:, (x - FIRST["x"]) % NX]
            blocks += [b[(y - FIRST["y"]) % NY] for y in range(NY)]
        whole = jnp.concatenate(blocks, 0)
        grad_proto[:, x * NC * SUB : (x + 1) * NC * SUB] = whole.T


def swap(x, axis, n, bit):
    return lax.ppermute(x, axis, [(i, i ^ bit) for i in range(n)])


def body(embeddings, prototypes):
    kept = lambda dtype: shape((G, 2, COLS, U), dtype)
    sums = shape((NY * NZ * 8, 128), bf16)
    acc = pltpu.VMEM((2 * COLS, 128), f32)

    rows, inverse, proto = pl.pallas_call(
        prepare_kernel,
        out_shape=(
            shape((NX, 2, U, 128), bf16),
            shape((2, U, 1), f32),
            shape((NZ, SUB, 128), bf16),
        ),
        in_specs=[pl.BlockSpec(memory_space=pltpu.HBM)] * 2,
        out_specs=(VM, VM, pl.BlockSpec(memory_space=pl.ANY)),
        scratch_shapes=[
            pltpu.VMEM((2, U, 128), bf16),
            pltpu.VMEM((128, 512), bf16),
            pltpu.VMEM((512, 128), f32),
            pltpu.VMEM((NZ, SUB, 128), bf16),
            pltpu.SemaphoreType.DMA((3,)),
        ],
        compiler_params=pltpu.CompilerParams(vmem_limit_bytes=20 * 1024 * 1024),
    )(*(pltpu.with_memory_space_constraint(a, pltpu.HBM) for a in (embeddings, prototypes)))
    mine = exchange(rows, ("x",))
    proto = exchange(proto, ("z",)).reshape(COLS, 128)
    other = swap(mine, "c", NC, 1)
    flat = call(flat_kernel, shape((128, COLS), bf16), proto, flops=1 << 36)
    proto, flat = lax.optimization_barrier((proto, flat))
    powered, masses, soft, columns = call(
        scores_kernel,
        (kept(bf16), kept(f32), shape((2 * G, U), f32), sums),
        mine,
        other,
        proto,
        scratch=[acc],
    )
    first = None
    for sweep in range(ITERS):
        columns = exchange(columns, ("y", "z"))
        lines = shape((G, 4 * G if sweep == 0 else 2 * G, U), bf16)
        mass = call(
            functools.partial(rows_kernel, sweep),
            (lines, shape((8, 128), f32)) if sweep == ITERS - 1 else lines,
            masses,
            columns,
            *((soft,) if sweep == 0 else ()),
            scratch=[acc],
        )
        if sweep == ITERS - 1:
            mass, scale = mass
        mass = exchange(mass, ("x", "c"))
        first = mass if first is None else first
        if sweep < ITERS - 1:
            columns = call(columns_kernel, sums, masses, mass, scratch=[acc])
    half = shape((2, 2, 128, U), bf16)
    stay, near, give_stay, give_near, parts = call(
        slopes_kernel,
        (half, half, half, half, shape((COLS, 128), f32)),
        mine,
        other,
        flat,
        powered,
        masses,
        scale,
        first,
        mass,
        scratch=[
            pltpu.VMEM((COLS, 128), f32),
            acc,
            pltpu.VMEM((4 * G, U), f32),
            pltpu.VMEM((2, COLS, 2 * U), bf16),
            pltpu.VMEM((NC, NX, 2, 128, U), bf16),
        ],
    )
    pieces = exchange(parts, ("y", "z"))
    near = call(add_kernel, half, near, swap(give_near, "c", NC, 1))
    other = swap(give_stay, "c", NC, 1)
    near = swap(near, "x", NX, 1)
    pieces = call(piece_kernel, shape((NY * NX * 8, 128), bf16), pieces, flops=1 << 36)
    whole = exchange(pieces, ("y", "x"))
    whole = lax.all_gather(whole, "c", axis=0)
    unit, far = call(
        near_kernel, (shape((2, 128, U), f32), shape((2, 128, U), bf16)), stay, other, near
    )
    far = swap(far, "x", NX, 3)
    return tuple(
        call(
            finish_kernel,
            (shape((2, U, 128), f32), shape((128, COLS), f32)),
            embeddings,
            inverse,
            unit,
            far,
            whole,
        )
    )


def solution(mesh):
    fine = Mesh(mesh.devices.reshape(NY, NX, NC, NZ), ("y", "x", "c", "z"))
    placed = (P(None, ("y", "x", "c", "z"), None), P(None, "z"))
    return jax.shard_map(
        body, mesh=fine, in_specs=placed, out_specs=placed, check_vma=False
    )
```

```python
import functools

import jax
import jax.numpy as jnp
from jax import lax
from jax.experimental import pallas as pl
from jax.experimental.pallas import tpu as pltpu
from jax.sharding import Mesh, PartitionSpec as P

K = 4096
ITERS = 3
SINK = 0.05
SHARP = 0.1

NY, NX, NC, NZ = 8, 4, 2, 8
G = NX * NC
U = 256
SUB = 512 // G
COLS = NZ * SUB
Q = COLS // 128
USERS = NY * NX * NC * NZ * U
EPS = 1e-06
f32, bf16 = jnp.float32, jnp.bfloat16
VM = pl.BlockSpec(memory_space=pltpu.VMEM)
shape = jax.ShapeDtypeStruct


SIZES = dict(y=NY, x=NX, c=NC, z=NZ)
FIRST = dict(y=4, x=2, c=1, z=4)
GATHER_FIRST = dict(z=0)


def order(axes, first=FIRST):
    places = [[]]
    for a in axes:
        places = [p + [(i + first[a]) % SIZES[a]] for p in places for i in range(SIZES[a])]
    return places


def exchange(x, axes, first=FIRST):
    members = []
    for place_ in order(axes, first):
        at = 0
        for a, i in zip(axes, place_):
            at = at * SIZES[a] + i
        members.append(at)
    axis = axes if len(axes) > 1 else axes[0]
    return lax.all_to_all(x, axis, 0, 0, tiled=True, axis_index_groups=[members])


def call(kernel, outs, *args, scratch=(), flops=0, aliases={}):
    cost = pl.CostEstimate(flops=flops, bytes_accessed=1 << 20, transcendentals=0) if flops else None
    return pl.pallas_call(
        kernel,
        out_shape=outs,
        in_specs=[VM] * len(args),
        out_specs=jax.tree.map(lambda _: VM, outs),
        scratch_shapes=list(scratch),
        cost_estimate=cost,
        input_output_aliases=aliases,
        compiler_params=pltpu.CompilerParams(vmem_limit_bytes=20 * 1024 * 1024),
    )(*args)


def fold(x):
    return jnp.sum(x.reshape(-1, 8, x.shape[-1]), 0)


def prepare_kernel(
    embeddings, prototypes, unit, inverse, proto, users, columns, turned, copies, sems
):
    fetch = [
        pltpu.make_async_copy(src, dst, sems.at[i])
        for i, (src, dst) in enumerate(((prototypes, columns), (embeddings, users)))
    ]
    for copy in fetch:
        copy.start()
    fetch[0].wait()
    turned[...] = columns[...].astype(f32).T
    j = lax.axis_index("x") * NC + lax.axis_index("c")
    own = turned[pl.ds(pl.multiple_of(j * SUB, SUB), SUB), :]
    own = (own * lax.rsqrt(jnp.sum(own * own, -1, keepdims=True) + EPS)).astype(bf16)
    for i in range(NZ):
        copies[i] = own
    leave = pltpu.make_async_copy(copies, proto, sems.at[2])
    leave.start()
    fetch[1].wait()
    for v in range(2):
        e = users[v].astype(f32)
        inv = lax.rsqrt(jnp.sum(e * e, -1, keepdims=True) + EPS)
        inverse[v] = inv
        unit[v] = (e * inv).astype(bf16)
    leave.wait()


def send_columns(acc, out):
    rows = [jnp.sum(acc[i * 128 : (i + 1) * 128, :].T, 0, keepdims=True) for i in range(2 * Q)]
    part = jnp.concatenate(rows, 0)
    out[...] = jnp.concatenate([part] * (NY * NZ), 0).astype(out.dtype)


def members(step):
    def member(r, _):
        step(r)
        return 0

    lax.fori_loop(0, NX, member, 0, unroll=True)


def place(half, r):
    return lax.rem(lax.axis_index("c") + half, NC) * NX + (lax.axis_index("x") ^ r)


def scores_kernel(half, rows, proto, *refs):
    powered, masses, soft, acc = refs if half == 0 else refs[4:8]
    if half == 0:
        acc[...] = jnp.zeros_like(acc)

    def group(r):
        g = place(half, r)
        for v in range(2):
            rowsum = jnp.zeros((8, U), f32)
            for q in range(COLS // 256):
                at = slice(q * 256, (q + 1) * 256)
                s = lax.dot_general(
                    proto[at, :], rows[r, v], (((1,), (1,)), ((), ())), preferred_element_type=f32
                )
                e = jnp.exp(s * (1.0 / SHARP))
                k = e * e
                powered[g, v, at, :] = e.astype(bf16)
                masses[g, v, at, :] = k
                rowsum += fold(e)
                acc[v * COLS + q * 256 : v * COLS + (q + 1) * 256, :] += k[:, :128] + k[:, 128:]
            soft[pl.ds(v * G + g, 1), :] = jnp.sum(rowsum, 0, keepdims=True)

    members(group)
    if half:
        send_columns(acc, refs[-1])


def rows_kernel(sweep, masses, columns, *refs):
    soft = refs[0] if sweep == 0 else None
    out, wide = refs[-2 if sweep < ITERS - 1 else -3], refs[-1]
    c = 1.0 / (K * fold(columns[...].astype(f32)))
    if sweep == ITERS - 1:
        refs[-2][...] = c
    turned = jnp.concatenate([c] * 16, 0).T
    for i in range(2 * Q):
        wide[i * 128 : (i + 1) * 128, :] = jnp.broadcast_to(turned[:, i : i + 1], (128, 128))
    lines = []
    for v in range(2):

        def eight(s, acc):
            at = pl.multiple_of(s * 8, 8)
            cc = wide[pl.ds(v * COLS + at, 8), :]
            cc = jnp.concatenate([cc, cc], 1)
            return tuple(acc[g] + masses[g, v, pl.ds(at, 8), :] * cc for g in range(G))

        acc = lax.fori_loop(0, COLS // 8, eight, (jnp.zeros((8, U), f32),) * G, unroll=16)
        lines += [jnp.sum(a, 0, keepdims=True) for a in acc]
    if soft is not None:
        lines.append(soft[...])
    out[0] = jnp.concatenate(lines, 0).astype(bf16)
    for i in range(1, G):
        out[i] = out[0]


def row_total(ref, first, n):
    return jnp.sum(ref[:, first : first + n, :].astype(f32), 0)


def columns_kernel(masses, rowmass, columns, acc):
    r = 1.0 / (USERS * row_total(rowmass, 0, 2 * G))
    for v in range(2):
        scale = [jnp.broadcast_to(r[v * G + g : v * G + g + 1, :], (8, U)) for g in range(G)]

        def eight(s, _):
            at = pl.multiple_of(s * 8, 8)
            total = masses[0, v, pl.ds(at, 8), :] * scale[0]
            for g in range(1, G):
                total += masses[g, v, pl.ds(at, 8), :] * scale[g]
            acc[pl.ds(v * COLS + at, 8), :] = total[:, :128] + total[:, 128:]
            return 0

        lax.fori_loop(0, COLS // 8, eight, 0, unroll=16)
    send_columns(acc, columns)


def flat_kernel(proto, flat):
    flat[...] = proto[...].astype(f32).T.astype(bf16)


def slopes_kernel(
    mine,
    other,
    flat,
    powered,
    masses,
    scale,
    first,
    last,
    stay,
    near,
    give_stay,
    give_near,
    parts,
    acc,
    wide,
    ab,
    slopes,
    units,
):
    acc[...] = jnp.zeros_like(acc)
    turned = jnp.concatenate([scale[...] * (1.0 / SHARP)] * 16, 0).T
    for i in range(2 * Q):
        wide[i * 128 : (i + 1) * 128, :] = jnp.broadcast_to(turned[:, i : i + 1], (128, 128))
    ab[0 : 2 * G, :] = (1.0 / SHARP) / row_total(first, 2 * G, 2 * G)
    ab[2 * G :, :] = 1.0 / row_total(last, 0, 2 * G)

    def group(half, r, rows):
        g = place(half, r)
        slot = ((r << 1) & 3) ^ ((r >> 1) * 3)
        slope = slopes.at[r % 2]
        for v in range(2):
            w = 1 - v
            a = ab[pl.ds(v * G + g, 1), :]
            b = ab[pl.ds(2 * G + w * G + g, 1), :]
            for q in range(Q):
                at = slice(q * 128, (q + 1) * 128)
                c = wide[(w * Q + q) * 128 : (w * Q + q + 1) * 128, :]
                slope[at, v * U : (v + 1) * U] = (
                    powered[g, v, at, :].astype(f32) * a
                    - masses[g, w, at, :] * jnp.concatenate([c, c], 1) * b
                ).astype(bf16)
        made = jnp.dot(flat[...], slope[...], preferred_element_type=f32).astype(bf16)
        for v in range(2):
            units[half, slot, v] = made[:, v * U : (v + 1) * U]
        acc[...] += jnp.dot(slope[...], rows[r].reshape(2 * U, 128), preferred_element_type=f32)

    for half, rows in enumerate((mine, other)):
        members(lambda r, half=half, rows=rows: group(half, r, rows))
    for i in range(2):
        for v in range(2):
            stay[v, i], near[v, i] = units[0, i, v], units[0, 2 + i, v]
            give_stay[v, i], give_near[v, i] = units[1, i, v], units[1, 2 + i, v]
    for i, (y, z) in enumerate(order(("y", "z"))):
        at = (z - GATHER_FIRST["z"]) % NZ * SUB + y * 8
        parts[i * 8 : (i + 1) * 8, :] = acc[at : at + 8, :]


def piece_kernel(pieces, out):
    out[...] = jnp.concatenate([fold(pieces[...])] * (NY * NX), 0).astype(bf16)


def add_kernel(mine, got, out):
    out[...] = (mine[...].astype(f32) + got[...].astype(f32)).astype(bf16)


def near_kernel(stay, other, got, unit, far):
    for v in range(2):
        unit[v] = stay[v, 0].astype(f32) + other[v, 0].astype(f32) + got[v, 0].astype(f32)
        last = stay[v, 1].astype(f32) + other[v, 1].astype(f32) + got[v, 1].astype(f32)
        far[v] = last.astype(bf16)


def finish_kernel(embeddings, inverse, kept, got, proto, grad_embed, grad_proto):
    for v in range(2):
        grad = (kept[v] + got[v].astype(f32)).T
        inv = inverse[v]
        unit = embeddings[v].astype(f32) * inv
        grad_embed[v] = inv * (grad - unit * jnp.sum(unit * grad, -1, keepdims=True))
    for x in range(NX):
        blocks = []
        for c in range(NC):
            b = proto[c].astype(f32).reshape(NY, NX, 8, 128)[:, (x - FIRST["x"]) % NX]
            blocks += [b[(y - FIRST["y"]) % NY] for y in range(NY)]
        whole = jnp.concatenate(blocks, 0)
        grad_proto[:, x * NC * SUB : (x + 1) * NC * SUB] = whole.T


def swap(x, axis, n, bit):
    return lax.ppermute(x, axis, [(i, i ^ bit) for i in range(n)])


def body(embeddings, prototypes):
    kept = lambda dtype: shape((G, 2, COLS, U), dtype)
    sums = shape((NY * NZ * 8, 128), bf16)
    acc = pltpu.VMEM((2 * COLS, 128), f32)

    unit, inverse, proto = pl.pallas_call(
        prepare_kernel,
        out_shape=(
            shape((2, U, 128), bf16),
            shape((2, U, 1), f32),
            shape((NZ, SUB, 128), bf16),
        ),
        in_specs=[pl.BlockSpec(memory_space=pltpu.HBM)] * 2,
        out_specs=(VM, VM, pl.BlockSpec(memory_space=pl.ANY)),
        scratch_shapes=[
            pltpu.VMEM((2, U, 128), bf16),
            pltpu.VMEM((128, 512), bf16),
            pltpu.VMEM((512, 128), f32),
            pltpu.VMEM((NZ, SUB, 128), bf16),
            pltpu.SemaphoreType.DMA((3,)),
        ],
        compiler_params=pltpu.CompilerParams(vmem_limit_bytes=20 * 1024 * 1024),
    )(*(pltpu.with_memory_space_constraint(a, pltpu.HBM) for a in (embeddings, prototypes)))
    proto = exchange(proto, ("z",), GATHER_FIRST).reshape(COLS, 128)
    others = [swap(unit, "x", NX, r) for r in range(1, NX)]
    flat = call(flat_kernel, shape((128, COLS), bf16), proto, flops=1 << 36)
    others, proto, flat = lax.optimization_barrier((others, proto, flat))
    mine = jnp.stack([unit] + others)
    other = swap(mine, "c", NC, 1)
    part = shape((2 * COLS, 128), f32)
    grid = (kept(bf16), kept(f32), shape((2 * G, U), f32))
    half = call(
        functools.partial(scores_kernel, 0),
        (*grid, part),
        mine,
        proto,
        flops=1 << 31,
    )
    powered, masses, soft, _, columns = call(
        functools.partial(scores_kernel, 1),
        (*grid, part, sums),
        other,
        proto,
        *half,
        aliases={2: 0, 3: 1, 4: 2, 5: 3},
    )
    first = None
    for sweep in range(ITERS):
        columns = exchange(columns, ("y", "z"))
        lines = shape((G, 4 * G if sweep == 0 else 2 * G, U), bf16)
        mass = call(
            functools.partial(rows_kernel, sweep),
            (lines, shape((8, 128), f32)) if sweep == ITERS - 1 else lines,
            masses,
            columns,
            *((soft,) if sweep == 0 else ()),
            scratch=[acc],
        )
        if sweep == ITERS - 1:
            mass, scale = mass
        mass = exchange(mass, ("x", "c"))
        first = mass if first is None else first
        if sweep < ITERS - 1:
            columns = call(columns_kernel, sums, masses, mass, scratch=[acc])
    half = shape((2, 2, 128, U), bf16)
    stay, near, give_stay, give_near, parts = call(
        slopes_kernel,
        (half, half, half, half, shape((COLS, 128), f32)),
        mine,
        other,
        flat,
        powered,
        masses,
        scale,
        first,
        mass,
        scratch=[
            pltpu.VMEM((COLS, 128), f32),
            acc,
            pltpu.VMEM((4 * G, U), f32),
            pltpu.VMEM((2, COLS, 2 * U), bf16),
            pltpu.VMEM((NC, NX, 2, 128, U), bf16),
        ],
    )
    pieces = exchange(parts, ("y", "z"))
    near = call(add_kernel, half, near, swap(give_near, "c", NC, 1))
    other = swap(give_stay, "c", NC, 1)
    near = swap(near, "x", NX, 1)
    pieces = call(piece_kernel, shape((NY * NX * 8, 128), bf16), pieces, flops=1 << 36)
    whole = exchange(pieces, ("y", "x"))
    whole = lax.all_gather(whole, "c", axis=0)
    unit, far = call(
        near_kernel, (shape((2, 128, U), f32), shape((2, 128, U), bf16)), stay, other, near
    )
    far = swap(far, "x", NX, 3)
    return tuple(
        call(
            finish_kernel,
            (shape((2, U, 128), f32), shape((128, COLS), f32)),
            embeddings,
            inverse,
            unit,
            far,
            whole,
        )
    )


def solution(mesh):
    fine = Mesh(mesh.devices.reshape(NY, NX, NC, NZ), ("y", "x", "c", "z"))
    placed = (P(None, ("y", "x", "c", "z"), None), P(None, "z"))
    return jax.shard_map(
        body, mesh=fine, in_specs=placed, out_specs=placed, check_vma=False
    )
```

```python
import functools

import jax
import jax.numpy as jnp
from jax import lax
from jax.experimental import pallas as pl
from jax.experimental.pallas import tpu as pltpu
from jax.sharding import Mesh, PartitionSpec as P

K = 4096
ITERS = 3
SINK = 0.05
SHARP = 0.1

NY, NX, NC, NZ = 8, 4, 2, 8
G = NX * NC
U = 256
SUB = 512 // G
COLS = NZ * SUB
Q = COLS // 128
USERS = NY * NX * NC * NZ * U
EPS = 1e-06
f32, bf16 = jnp.float32, jnp.bfloat16
VM = pl.BlockSpec(memory_space=pltpu.VMEM)
shape = jax.ShapeDtypeStruct


SIZES = dict(y=NY, x=NX, c=NC, z=NZ)
FIRST = dict(y=4, x=2, c=1, z=5)
GATHER_FIRST = dict(z=0)


def order(axes, first=FIRST):
    places = [[]]
    for a in axes:
        places = [p + [(i + first[a]) % SIZES[a]] for p in places for i in range(SIZES[a])]
    return places


def exchange(x, axes, first=FIRST):
    members = []
    for place_ in order(axes, first):
        at = 0
        for a, i in zip(axes, place_):
            at = at * SIZES[a] + i
        members.append(at)
    axis = axes if len(axes) > 1 else axes[0]
    return lax.all_to_all(x, axis, 0, 0, tiled=True, axis_index_groups=[members])


def call(kernel, outs, *args, scratch=(), flops=0, aliases={}):
    cost = pl.CostEstimate(flops=flops, bytes_accessed=1 << 20, transcendentals=0) if flops else None
    return pl.pallas_call(
        kernel,
        out_shape=outs,
        in_specs=[VM] * len(args),
        out_specs=jax.tree.map(lambda _: VM, outs),
        scratch_shapes=list(scratch),
        cost_estimate=cost,
        input_output_aliases=aliases,
        compiler_params=pltpu.CompilerParams(vmem_limit_bytes=20 * 1024 * 1024),
    )(*args)


def fold(x):
    return jnp.sum(x.reshape(-1, 8, x.shape[-1]), 0)


def prepare_kernel(
    embeddings, prototypes, unit, inverse, proto, users, columns, turned, copies, sems
):
    j = lax.axis_index("x") * NC + lax.axis_index("c")
    near = prototypes.at[:, pl.ds(pl.multiple_of(lax.div(j, 2) * 128, 128), 128)]
    fetch = [
        pltpu.make_async_copy(src, dst, sems.at[i])
        for i, (src, dst) in enumerate(((near, columns), (embeddings, users)))
    ]
    for copy in fetch:
        copy.start()
    fetch[0].wait()
    turned[...] = columns[...].astype(f32).T
    own = turned[pl.ds(pl.multiple_of(lax.rem(j, 2) * SUB, SUB), SUB), :]
    own = (own * lax.rsqrt(jnp.sum(own * own, -1, keepdims=True) + EPS)).astype(bf16)
    for i in range(NZ):
        copies[i] = own
    leave = pltpu.make_async_copy(copies, proto, sems.at[2])
    leave.start()
    fetch[1].wait()
    for v in range(2):
        e = users[v].astype(f32)
        inv = lax.rsqrt(jnp.sum(e * e, -1, keepdims=True) + EPS)
        inverse[v] = inv
        unit[v] = (e * inv).astype(bf16)
    leave.wait()


def send_columns(acc, out):
    rows = [jnp.sum(acc[i * 128 : (i + 1) * 128, :].T, 0, keepdims=True) for i in range(2 * Q)]
    part = jnp.concatenate(rows, 0)
    out[...] = jnp.concatenate([part] * (NY * NZ), 0).astype(out.dtype)


def members(step):
    def member(r, _):
        step(r)
        return 0

    lax.fori_loop(0, NX, member, 0, unroll=True)


def place(half, r):
    return lax.rem(lax.axis_index("c") + half, NC) * NX + (lax.axis_index("x") ^ r)


def scores_kernel(half, rows, proto, *refs):
    powered, masses, soft, acc = refs if half == 0 else refs[4:8]
    if half == 0:
        acc[...] = jnp.zeros_like(acc)

    def group(r):
        g = place(half, r)
        for v in range(2):
            rowsum = jnp.zeros((8, U), f32)
            for q in range(COLS // 256):
                at = slice(q * 256, (q + 1) * 256)
                s = lax.dot_general(
                    proto[at, :], rows[r, v], (((1,), (1,)), ((), ())), preferred_element_type=f32
                )
                e = jnp.exp(s * (1.0 / SHARP))
                k = e * e
                powered[g, v, at, :] = e.astype(bf16)
                masses[g, v, at, :] = k
                rowsum += fold(e)
                acc[v * COLS + q * 256 : v * COLS + (q + 1) * 256, :] += k[:, :128] + k[:, 128:]
            soft[pl.ds(v * G + g, 1), :] = jnp.sum(rowsum, 0, keepdims=True)

    members(group)
    if half:
        send_columns(acc, refs[-1])


def rows_kernel(sweep, masses, columns, *refs):
    soft = refs[0] if sweep == 0 else None
    out, wide = refs[-2 if sweep < ITERS - 1 else -3], refs[-1]
    c = 1.0 / (K * fold(columns[...].astype(f32)))
    if sweep == ITERS - 1:
        refs[-2][...] = c
    turned = jnp.concatenate([c] * 16, 0).T
    for i in range(2 * Q):
        wide[i * 128 : (i + 1) * 128, :] = jnp.broadcast_to(turned[:, i : i + 1], (128, 128))
    lines = []
    for v in range(2):

        def eight(s, acc):
            at = pl.multiple_of(s * 8, 8)
            cc = wide[pl.ds(v * COLS + at, 8), :]
            cc = jnp.concatenate([cc, cc], 1)
            return tuple(acc[g] + masses[g, v, pl.ds(at, 8), :] * cc for g in range(G))

        acc = lax.fori_loop(0, COLS // 8, eight, (jnp.zeros((8, U), f32),) * G, unroll=32)
        lines += [jnp.sum(a, 0, keepdims=True) for a in acc]
    if soft is not None:
        lines.append(soft[...])
    out[0] = jnp.concatenate(lines, 0).astype(bf16)
    for i in range(1, G):
        out[i] = out[0]


def row_total(ref, first, n):
    return jnp.sum(ref[:, first : first + n, :].astype(f32), 0)


def columns_kernel(masses, rowmass, columns, acc):
    r = 1.0 / (USERS * row_total(rowmass, 0, 2 * G))
    for v in range(2):
        scale = [jnp.broadcast_to(r[v * G + g : v * G + g + 1, :], (8, U)) for g in range(G)]

        def eight(s, _):
            at = pl.multiple_of(s * 8, 8)
            total = masses[0, v, pl.ds(at, 8), :] * scale[0]
            for g in range(1, G):
                total += masses[g, v, pl.ds(at, 8), :] * scale[g]
            acc[pl.ds(v * COLS + at, 8), :] = total[:, :128] + total[:, 128:]
            return 0

        lax.fori_loop(0, COLS // 8, eight, 0, unroll=32)
    send_columns(acc, columns)


def flat_kernel(proto, flat):
    flat[...] = proto[...].astype(f32).T.astype(bf16)


def slopes_kernel(
    mine,
    other,
    flat,
    powered,
    masses,
    scale,
    first,
    last,
    stay,
    near,
    give_stay,
    give_near,
    parts,
    acc,
    wide,
    ab,
    slopes,
    units,
):
    acc[...] = jnp.zeros_like(acc)
    turned = jnp.concatenate([scale[...] * (1.0 / SHARP)] * 16, 0).T
    for i in range(2 * Q):
        wide[i * 128 : (i + 1) * 128, :] = jnp.broadcast_to(turned[:, i : i + 1], (128, 128))
    ab[0 : 2 * G, :] = (1.0 / SHARP) / row_total(first, 2 * G, 2 * G)
    ab[2 * G :, :] = 1.0 / row_total(last, 0, 2 * G)

    def group(half, r, rows):
        g = place(half, r)
        slot = ((r << 1) & 3) ^ ((r >> 1) * 3)
        slope = slopes.at[r % 2]
        for v in range(2):
            w = 1 - v
            a = ab[pl.ds(v * G + g, 1), :]
            b = ab[pl.ds(2 * G + w * G + g, 1), :]
            for q in range(Q):
                at = slice(q * 128, (q + 1) * 128)
                c = wide[(w * Q + q) * 128 : (w * Q + q + 1) * 128, :]
                slope[at, v * U : (v + 1) * U] = (
                    powered[g, v, at, :].astype(f32) * a
                    - masses[g, w, at, :] * jnp.concatenate([c, c], 1) * b
                ).astype(bf16)
        made = jnp.dot(flat[...], slope[...], preferred_element_type=f32).astype(bf16)
        for v in range(2):
            units[half, slot, v] = made[:, v * U : (v + 1) * U]
        acc[...] += jnp.dot(slope[...], rows[r].reshape(2 * U, 128), preferred_element_type=f32)

    for half, rows in enumerate((mine, other)):
        members(lambda r, half=half, rows=rows: group(half, r, rows))
    for i in range(2):
        for v in range(2):
            stay[v, i], near[v, i] = units[0, i, v], units[0, 2 + i, v]
            give_stay[v, i], give_near[v, i] = units[1, i, v], units[1, 2 + i, v]
    for i, (y, z) in enumerate(order(("y", "z"))):
        at = (z - GATHER_FIRST["z"]) % NZ * SUB + y * 8
        parts[i * 8 : (i + 1) * 8, :] = acc[at : at + 8, :]


def piece_kernel(pieces, out):
    out[...] = jnp.concatenate([fold(pieces[...])] * (NY * NX), 0).astype(bf16)


def add_kernel(mine, got, out):
    out[...] = (mine[...].astype(f32) + got[...].astype(f32)).astype(bf16)


def near_kernel(stay, other, got, unit, far):
    for v in range(2):
        unit[v] = stay[v, 0].astype(f32) + other[v, 0].astype(f32) + got[v, 0].astype(f32)
        last = stay[v, 1].astype(f32) + other[v, 1].astype(f32) + got[v, 1].astype(f32)
        far[v] = last.astype(bf16)


def finish_kernel(embeddings, inverse, kept, got, proto, grad_embed, grad_proto):
    for v in range(2):
        grad = (kept[v] + got[v].astype(f32)).T
        inv = inverse[v]
        unit = embeddings[v].astype(f32) * inv
        grad_embed[v] = inv * (grad - unit * jnp.sum(unit * grad, -1, keepdims=True))
    for x in range(NX):
        blocks = []
        for c in range(NC):
            b = proto[c].astype(f32).reshape(NY, NX, 8, 128)[:, (x - FIRST["x"]) % NX]
            blocks += [b[(y - FIRST["y"]) % NY] for y in range(NY)]
        whole = jnp.concatenate(blocks, 0)
        grad_proto[:, x * NC * SUB : (x + 1) * NC * SUB] = whole.T


def swap(x, axis, n, bit):
    return lax.ppermute(x, axis, [(i, i ^ bit) for i in range(n)])


def body(embeddings, prototypes):
    kept = lambda dtype: shape((G, 2, COLS, U), dtype)
    sums = shape((NY * NZ * 8, 128), bf16)
    acc = pltpu.VMEM((2 * COLS, 128), f32)

    unit, inverse, proto = pl.pallas_call(
        prepare_kernel,
        out_shape=(
            shape((2, U, 128), bf16),
            shape((2, U, 1), f32),
            shape((NZ, SUB, 128), bf16),
        ),
        in_specs=[pl.BlockSpec(memory_space=pltpu.HBM)] * 2,
        out_specs=(VM, VM, pl.BlockSpec(memory_space=pl.ANY)),
        scratch_shapes=[
            pltpu.VMEM((2, U, 128), bf16),
            pltpu.VMEM((128, 128), bf16),
            pltpu.VMEM((128, 128), f32),
            pltpu.VMEM((NZ, SUB, 128), bf16),
            pltpu.SemaphoreType.DMA((3,)),
        ],
        compiler_params=pltpu.CompilerParams(vmem_limit_bytes=20 * 1024 * 1024),
    )(*(pltpu.with_memory_space_constraint(a, pltpu.HBM) for a in (embeddings, prototypes)))
    proto = exchange(proto, ("z",), GATHER_FIRST).reshape(COLS, 128)
    others = [swap(unit, "x", NX, r) for r in range(1, NX)]
    flat = call(flat_kernel, shape((128, COLS), bf16), proto, flops=1 << 36)
    others, proto, flat = lax.optimization_barrier((others, proto, flat))
    mine = jnp.stack([unit] + others)
    other = swap(mine, "c", NC, 1)
    part = shape((2 * COLS, 128), f32)
    grid = (kept(bf16), kept(f32), shape((2 * G, U), f32))
    half = call(
        functools.partial(scores_kernel, 0),
        (*grid, part),
        mine,
        proto,
        flops=1 << 31,
    )
    powered, masses, soft, _, columns = call(
        functools.partial(scores_kernel, 1),
        (*grid, part, sums),
        other,
        proto,
        *half,
        aliases={2: 0, 3: 1, 4: 2, 5: 3},
    )
    first = None
    for sweep in range(ITERS):
        columns = exchange(columns, ("y", "z"))
        lines = shape((G, 4 * G if sweep == 0 else 2 * G, U), bf16)
        mass = call(
            functools.partial(rows_kernel, sweep),
            (lines, shape((8, 128), f32)) if sweep == ITERS - 1 else lines,
            masses,
            columns,
            *((soft,) if sweep == 0 else ()),
            scratch=[acc],
        )
        if sweep == ITERS - 1:
            mass, scale = mass
        mass = exchange(mass, ("x", "c"))
        first = mass if first is None else first
        if sweep < ITERS - 1:
            columns = call(columns_kernel, sums, masses, mass, scratch=[acc])
    half = shape((2, 2, 128, U), bf16)
    stay, near, give_stay, give_near, parts = call(
        slopes_kernel,
        (half, half, half, half, shape((COLS, 128), f32)),
        mine,
        other,
        flat,
        powered,
        masses,
        scale,
        first,
        mass,
        scratch=[
            pltpu.VMEM((COLS, 128), f32),
            acc,
            pltpu.VMEM((4 * G, U), f32),
            pltpu.VMEM((2, COLS, 2 * U), bf16),
            pltpu.VMEM((NC, NX, 2, 128, U), bf16),
        ],
    )
    pieces = exchange(parts, ("y", "z"))
    near = call(add_kernel, half, near, swap(give_near, "c", NC, 1))
    other = swap(give_stay, "c", NC, 1)
    near = swap(near, "x", NX, 1)
    pieces = call(piece_kernel, shape((NY * NX * 8, 128), bf16), pieces, flops=1 << 36)
    whole = exchange(pieces, ("y", "x"))
    whole = lax.all_gather(whole, "c", axis=0)
    unit, far = call(
        near_kernel, (shape((2, 128, U), f32), shape((2, 128, U), bf16)), stay, other, near
    )
    far = swap(far, "x", NX, 3)
    return tuple(
        call(
            finish_kernel,
            (shape((2, U, 128), f32), shape((128, COLS), f32)),
            embeddings,
            inverse,
            unit,
            far,
            whole,
        )
    )


def solution(mesh):
    fine = Mesh(mesh.devices.reshape(NY, NX, NC, NZ), ("y", "x", "c", "z"))
    placed = (P(None, ("y", "x", "c", "z"), None), P(None, "z"))
    return jax.shard_map(
        body, mesh=fine, in_specs=placed, out_specs=placed, check_vma=False
    )
```

```python
import functools

import jax
import jax.numpy as jnp
from jax import lax
from jax.experimental import pallas as pl
from jax.experimental.pallas import tpu as pltpu
from jax.sharding import Mesh, PartitionSpec as P

K = 4096
ITERS = 3
SINK = 0.05
SHARP = 0.1

NY, NX, NC, NZ = 8, 4, 2, 8
G = NX * NC
U = 256
SUB = 512 // G
COLS = NZ * SUB
Q = COLS // 128
USERS = NY * NX * NC * NZ * U
EPS = 1e-06
f32, bf16 = jnp.float32, jnp.bfloat16
VM = pl.BlockSpec(memory_space=pltpu.VMEM)
shape = jax.ShapeDtypeStruct


SIZES = dict(y=NY, x=NX, c=NC, z=NZ)
FIRST = dict(y=4, x=2, c=1, z=5)
GATHER_FIRST = dict(z=0)


def order(axes, first=FIRST):
    places = [[]]
    for a in axes:
        places = [p + [(i + first[a]) % SIZES[a]] for p in places for i in range(SIZES[a])]
    return places


def exchange(x, axes, first=FIRST):
    members = []
    for place_ in order(axes, first):
        at = 0
        for a, i in zip(axes, place_):
            at = at * SIZES[a] + i
        members.append(at)
    axis = axes if len(axes) > 1 else axes[0]
    return lax.all_to_all(x, axis, 0, 0, tiled=True, axis_index_groups=[members])


def call(kernel, outs, *args, scratch=(), flops=0, aliases={}):
    cost = pl.CostEstimate(flops=flops, bytes_accessed=1 << 20, transcendentals=0) if flops else None
    return pl.pallas_call(
        kernel,
        out_shape=outs,
        in_specs=[VM] * len(args),
        out_specs=jax.tree.map(lambda _: VM, outs),
        scratch_shapes=list(scratch),
        cost_estimate=cost,
        input_output_aliases=aliases,
        compiler_params=pltpu.CompilerParams(vmem_limit_bytes=20 * 1024 * 1024),
    )(*args)


def fold(x):
    return jnp.sum(x.reshape(-1, 8, x.shape[-1]), 0)


def prepare_kernel(
    embeddings, prototypes, unit, inverse, proto, users, columns, turned, copies, sems
):
    j = lax.axis_index("x") * NC + lax.axis_index("c")
    near = prototypes.at[:, pl.ds(pl.multiple_of(lax.div(j, 2) * 128, 128), 128)]
    fetch = [
        pltpu.make_async_copy(src, dst, sems.at[i])
        for i, (src, dst) in enumerate(((near, columns), (embeddings, users)))
    ]
    for copy in fetch:
        copy.start()
    fetch[0].wait()
    turned[...] = columns[...].astype(f32).T
    own = turned[pl.ds(pl.multiple_of(lax.rem(j, 2) * SUB, SUB), SUB), :]
    own = (own * lax.rsqrt(jnp.sum(own * own, -1, keepdims=True) + EPS)).astype(bf16)
    for i in range(NZ):
        copies[i] = own
    leave = pltpu.make_async_copy(copies, proto, sems.at[2])
    leave.start()
    fetch[1].wait()
    for v in range(2):
        e = users[v].astype(f32)
        inv = lax.rsqrt(jnp.sum(e * e, -1, keepdims=True) + EPS)
        inverse[v] = inv
        unit[v] = (e * inv).astype(bf16)
    leave.wait()


def send_columns(acc, out):
    rows = [jnp.sum(acc[i * 128 : (i + 1) * 128, :].T, 0, keepdims=True) for i in range(2 * Q)]
    part = jnp.concatenate(rows, 0)
    out[...] = jnp.concatenate([part] * (NY * NZ), 0).astype(out.dtype)


def members(step):
    def member(r, _):
        step(r)
        return 0

    lax.fori_loop(0, NX, member, 0, unroll=True)


def place(half, r):
    return lax.rem(lax.axis_index("c") + half, NC) * NX + (lax.axis_index("x") ^ r)


def scores_kernel(half, rows, proto, *refs):
    powered, masses, soft, acc = refs if half == 0 else refs[4:8]
    if half == 0:
        acc[...] = jnp.zeros_like(acc)

    def group(r):
        g = place(half, r)
        for v in range(2):
            rowsum = jnp.zeros((8, U), f32)
            for q in range(COLS // 256):
                at = slice(q * 256, (q + 1) * 256)
                s = lax.dot_general(
                    proto[at, :], rows[r, v], (((1,), (1,)), ((), ())), preferred_element_type=f32
                )
                e = jnp.exp(s * (1.0 / SHARP))
                k = e * e
                powered[g, v, at, :] = e.astype(bf16)
                masses[g, v, at, :] = k
                rowsum += fold(e)
                acc[v * COLS + q * 256 : v * COLS + (q + 1) * 256, :] += k[:, :128] + k[:, 128:]
            soft[pl.ds(v * G + g, 1), :] = jnp.sum(rowsum, 0, keepdims=True)

    members(group)
    if half:
        send_columns(acc, refs[-1])


def rows_kernel(sweep, masses, columns, *refs):
    soft = refs[0] if sweep == 0 else None
    out, wide = refs[-2 if sweep < ITERS - 1 else -3], refs[-1]
    c = 1.0 / (K * fold(columns[...].astype(f32)))
    if sweep == ITERS - 1:
        refs[-2][...] = c
    turned = jnp.concatenate([c] * 16, 0).T
    for i in range(2 * Q):
        wide[i * 128 : (i + 1) * 128, :] = jnp.broadcast_to(turned[:, i : i + 1], (128, 128))
    lines = []
    for v in range(2):

        def eight(s, acc):
            at = pl.multiple_of(s * 8, 8)
            cc = wide[pl.ds(v * COLS + at, 8), :]
            cc = jnp.concatenate([cc, cc], 1)
            return tuple(acc[g] + masses[g, v, pl.ds(at, 8), :] * cc for g in range(G))

        acc = lax.fori_loop(0, COLS // 8, eight, (jnp.zeros((8, U), f32),) * G, unroll=32)
        lines += [jnp.sum(a, 0, keepdims=True) for a in acc]
    if soft is not None:
        lines.append(soft[...])
    out[0] = jnp.concatenate(lines, 0).astype(bf16)
    for i in range(1, G):
        out[i] = out[0]


def row_total(ref, first, n):
    return jnp.sum(ref[:, first : first + n, :].astype(f32), 0)


def columns_kernel(masses, rowmass, columns, acc):
    r = 1.0 / (USERS * row_total(rowmass, 0, 2 * G))
    for v in range(2):
        scale = [jnp.broadcast_to(r[v * G + g : v * G + g + 1, :], (8, U)) for g in range(G)]

        def eight(s, _):
            at = pl.multiple_of(s * 8, 8)
            total = masses[0, v, pl.ds(at, 8), :] * scale[0]
            for g in range(1, G):
                total += masses[g, v, pl.ds(at, 8), :] * scale[g]
            acc[pl.ds(v * COLS + at, 8), :] = total[:, :128] + total[:, 128:]
            return 0

        lax.fori_loop(0, COLS // 8, eight, 0, unroll=32)
    send_columns(acc, columns)


def flat_kernel(proto, flat):
    flat[...] = proto[...].astype(f32).T.astype(bf16)


def slopes_kernel(
    mine,
    other,
    flat,
    powered,
    masses,
    scale,
    first,
    last,
    stay,
    near,
    give_stay,
    give_near,
    parts,
    acc,
    wide,
    ab,
    slopes,
):
    acc[...] = jnp.zeros_like(acc)
    turned = jnp.concatenate([scale[...] * (1.0 / SHARP)] * 16, 0).T
    for i in range(2 * Q):
        wide[i * 128 : (i + 1) * 128, :] = jnp.broadcast_to(turned[:, i : i + 1], (128, 128))
    ab[0 : 2 * G, :] = (1.0 / SHARP) / row_total(first, 2 * G, 2 * G)
    ab[2 * G :, :] = 1.0 / row_total(last, 0, 2 * G)

    def group(half, r, rows):
        g = place(half, r)
        slot = ((r << 1) & 3) ^ ((r >> 1) * 3)
        slope = slopes.at[r % 2]
        for v in range(2):
            w = 1 - v
            a = ab[pl.ds(v * G + g, 1), :]
            b = ab[pl.ds(2 * G + w * G + g, 1), :]
            for q in range(Q):
                at = slice(q * 128, (q + 1) * 128)
                c = wide[(w * Q + q) * 128 : (w * Q + q + 1) * 128, :]
                slope[at, v * U : (v + 1) * U] = (
                    powered[g, v, at, :].astype(f32) * a
                    - masses[g, w, at, :] * jnp.concatenate([c, c], 1) * b
                ).astype(bf16)
        made = jnp.dot(flat[...], slope[...], preferred_element_type=f32).astype(bf16)
        for v in range(2):
            out = (give_stay, give_near) if half else (stay, near)
            out[slot // 2][v, slot % 2] = made[:, v * U : (v + 1) * U]
        acc[...] += jnp.dot(slope[...], rows[r].reshape(2 * U, 128), preferred_element_type=f32)

    for half, rows in enumerate((mine, other)):
        for r in range(NX):
            group(half, r, rows)
    for i, (y, z) in enumerate(order(("y", "z"))):
        at = (z - GATHER_FIRST["z"]) % NZ * SUB + y * 8
        parts[i * 8 : (i + 1) * 8, :] = acc[at : at + 8, :]


def piece_kernel(pieces, out):
    out[...] = jnp.concatenate([fold(pieces[...])] * (NY * NX), 0).astype(bf16)


def add_kernel(mine, got, out):
    out[...] = (mine[...].astype(f32) + got[...].astype(f32)).astype(bf16)


def near_kernel(stay, other, got, unit, far):
    for v in range(2):
        unit[v] = stay[v, 0].astype(f32) + other[v, 0].astype(f32) + got[v, 0].astype(f32)
        last = stay[v, 1].astype(f32) + other[v, 1].astype(f32) + got[v, 1].astype(f32)
        far[v] = last.astype(bf16)


def finish_kernel(embeddings, inverse, kept, got, proto, grad_embed, grad_proto):
    for v in range(2):
        grad = (kept[v] + got[v].astype(f32)).T
        inv = inverse[v]
        unit = embeddings[v].astype(f32) * inv
        grad_embed[v] = inv * (grad - unit * jnp.sum(unit * grad, -1, keepdims=True))
    for x in range(NX):
        blocks = []
        for c in range(NC):
            b = proto[c].astype(f32).reshape(NY, NX, 8, 128)[:, (x - FIRST["x"]) % NX]
            blocks += [b[(y - FIRST["y"]) % NY] for y in range(NY)]
        whole = jnp.concatenate(blocks, 0)
        grad_proto[:, x * NC * SUB : (x + 1) * NC * SUB] = whole.T


def swap(x, axis, n, bit):
    return lax.ppermute(x, axis, [(i, i ^ bit) for i in range(n)])


def body(embeddings, prototypes):
    kept = lambda dtype: shape((G, 2, COLS, U), dtype)
    sums = shape((NY * NZ * 8, 128), bf16)
    acc = pltpu.VMEM((2 * COLS, 128), f32)

    unit, inverse, proto = pl.pallas_call(
        prepare_kernel,
        out_shape=(
            shape((2, U, 128), bf16),
            shape((2, U, 1), f32),
            shape((NZ, SUB, 128), bf16),
        ),
        in_specs=[pl.BlockSpec(memory_space=pltpu.HBM)] * 2,
        out_specs=(VM, VM, pl.BlockSpec(memory_space=pl.ANY)),
        scratch_shapes=[
            pltpu.VMEM((2, U, 128), bf16),
            pltpu.VMEM((128, 128), bf16),
            pltpu.VMEM((128, 128), f32),
            pltpu.VMEM((NZ, SUB, 128), bf16),
            pltpu.SemaphoreType.DMA((3,)),
        ],
        compiler_params=pltpu.CompilerParams(vmem_limit_bytes=20 * 1024 * 1024),
    )(*(pltpu.with_memory_space_constraint(a, pltpu.HBM) for a in (embeddings, prototypes)))
    proto = exchange(proto, ("z",), GATHER_FIRST).reshape(COLS, 128)
    others = [swap(unit, "x", NX, r) for r in range(1, NX)]
    flat = call(flat_kernel, shape((128, COLS), bf16), proto, flops=1 << 36)
    others, proto, flat = lax.optimization_barrier((others, proto, flat))
    mine = jnp.stack([unit] + others)
    other = swap(mine, "c", NC, 1)
    part = shape((2 * COLS, 128), f32)
    grid = (kept(bf16), kept(f32), shape((2 * G, U), f32))
    half = call(
        functools.partial(scores_kernel, 0),
        (*grid, part),
        mine,
        proto,
        flops=1 << 31,
    )
    powered, masses, soft, _, columns = call(
        functools.partial(scores_kernel, 1),
        (*grid, part, sums),
        other,
        proto,
        *half,
        aliases={2: 0, 3: 1, 4: 2, 5: 3},
    )
    first = None
    for sweep in range(ITERS):
        columns = exchange(columns, ("y", "z"))
        lines = shape((G, 4 * G if sweep == 0 else 2 * G, U), bf16)
        mass = call(
            functools.partial(rows_kernel, sweep),
            (lines, shape((8, 128), f32)) if sweep == ITERS - 1 else lines,
            masses,
            columns,
            *((soft,) if sweep == 0 else ()),
            scratch=[acc],
        )
        if sweep == ITERS - 1:
            mass, scale = mass
        mass = exchange(mass, ("x", "c"))
        first = mass if first is None else first
        if sweep < ITERS - 1:
            columns = call(columns_kernel, sums, masses, mass, scratch=[acc])
    half = shape((2, 2, 128, U), bf16)
    stay, near, give_stay, give_near, parts = call(
        slopes_kernel,
        (half, half, half, half, shape((COLS, 128), f32)),
        mine,
        other,
        flat,
        powered,
        masses,
        scale,
        first,
        mass,
        scratch=[
            pltpu.VMEM((COLS, 128), f32),
            acc,
            pltpu.VMEM((4 * G, U), f32),
            pltpu.VMEM((2, COLS, 2 * U), bf16),
        ],
    )
    pieces = exchange(parts, ("y", "z"))
    near = call(add_kernel, half, near, swap(give_near, "c", NC, 1))
    other = swap(give_stay, "c", NC, 1)
    near = swap(near, "x", NX, 1)
    pieces = call(piece_kernel, shape((NY * NX * 8, 128), bf16), pieces, flops=1 << 36)
    whole = exchange(pieces, ("y", "x"))
    whole = lax.all_gather(whole, "c", axis=0)
    unit, far = call(
        near_kernel, (shape((2, 128, U), f32), shape((2, 128, U), bf16)), stay, other, near
    )
    far = swap(far, "x", NX, 3)
    return tuple(
        call(
            finish_kernel,
            (shape((2, U, 128), f32), shape((128, COLS), f32)),
            embeddings,
            inverse,
            unit,
            far,
            whole,
        )
    )


def solution(mesh):
    fine = Mesh(mesh.devices.reshape(NY, NX, NC, NZ), ("y", "x", "c", "z"))
    placed = (P(None, ("y", "x", "c", "z"), None), P(None, "z"))
    return jax.shard_map(
        body, mesh=fine, in_specs=placed, out_specs=placed, check_vma=False
    )
```

```python
import functools

import jax
import jax.numpy as jnp
from jax import lax
from jax.experimental import pallas as pl
from jax.experimental.pallas import tpu as pltpu
from jax.sharding import Mesh, PartitionSpec as P

K = 4096
ITERS = 3
SINK = 0.05
SHARP = 0.1

NY, NX, NC, NZ = 8, 4, 2, 8
G = NX * NC
U = 256
SUB = 512 // G
COLS = NZ * SUB
Q = COLS // 128
USERS = NY * NX * NC * NZ * U
EPS = 1e-06
f32, bf16 = jnp.float32, jnp.bfloat16
VM = pl.BlockSpec(memory_space=pltpu.VMEM)
shape = jax.ShapeDtypeStruct


SIZES = dict(y=NY, x=NX, c=NC, z=NZ)
FIRST = dict(y=5, x=2, c=1, z=5)
GATHER_FIRST = dict(z=0)


def order(axes, first=FIRST):
    places = [[]]
    for a in axes:
        places = [p + [(i + first[a]) % SIZES[a]] for p in places for i in range(SIZES[a])]
    return places


def exchange(x, axes, first=FIRST):
    members = []
    for place_ in order(axes, first):
        at = 0
        for a, i in zip(axes, place_):
            at = at * SIZES[a] + i
        members.append(at)
    axis = axes if len(axes) > 1 else axes[0]
    return lax.all_to_all(x, axis, 0, 0, tiled=True, axis_index_groups=[members])


def call(kernel, outs, *args, scratch=(), flops=0, aliases={}):
    cost = pl.CostEstimate(flops=flops, bytes_accessed=1 << 20, transcendentals=0) if flops else None
    return pl.pallas_call(
        kernel,
        out_shape=outs,
        in_specs=[VM] * len(args),
        out_specs=jax.tree.map(lambda _: VM, outs),
        scratch_shapes=list(scratch),
        cost_estimate=cost,
        input_output_aliases=aliases,
        compiler_params=pltpu.CompilerParams(vmem_limit_bytes=20 * 1024 * 1024),
    )(*args)


def fold(x):
    return jnp.sum(x.reshape(-1, 8, x.shape[-1]), 0)


def prepare_kernel(
    embeddings, prototypes, unit, inverse, proto, users, columns, turned, copies, sems
):
    j = lax.axis_index("x") * NC + lax.axis_index("c")
    near = prototypes.at[:, pl.ds(pl.multiple_of(lax.div(j, 2) * 128, 128), 128)]
    fetch = [
        pltpu.make_async_copy(src, dst, sems.at[i])
        for i, (src, dst) in enumerate(((near, columns), (embeddings, users)))
    ]
    for copy in fetch:
        copy.start()
    fetch[0].wait()
    turned[...] = columns[...].astype(f32).T
    own = turned[pl.ds(pl.multiple_of(lax.rem(j, 2) * SUB, SUB), SUB), :]
    own = (own * lax.rsqrt(jnp.sum(own * own, -1, keepdims=True) + EPS)).astype(bf16)
    for i in range(NZ):
        copies[i] = own
    leave = pltpu.make_async_copy(copies, proto, sems.at[2])
    leave.start()
    fetch[1].wait()
    for v in range(2):
        e = users[v].astype(f32)
        inv = lax.rsqrt(jnp.sum(e * e, -1, keepdims=True) + EPS)
        inverse[v] = inv
        unit[v] = (e * inv).astype(bf16)
    leave.wait()


def send_columns(acc, out):
    rows = [jnp.sum(acc[i * 128 : (i + 1) * 128, :].T, 0, keepdims=True) for i in range(2 * Q)]
    part = jnp.concatenate(rows, 0)
    out[...] = jnp.concatenate([part] * (NY * NZ), 0).astype(out.dtype)


def members(step):
    def member(r, _):
        step(r)
        return 0

    lax.fori_loop(0, NX, member, 0, unroll=True)


def place(half, r):
    return lax.rem(lax.axis_index("c") + half, NC) * NX + (lax.axis_index("x") ^ r)


def scores_kernel(half, rows, proto, *refs):
    powered, masses, soft, acc = refs if half == 0 else refs[4:8]
    if half == 0:
        acc[...] = jnp.zeros_like(acc)

    def group(r):
        g = place(half, r)
        for v in range(2):
            rowsum = jnp.zeros((8, U), f32)
            for q in range(COLS // 256):
                at = slice(q * 256, (q + 1) * 256)
                s = lax.dot_general(
                    proto[at, :], rows[r, v], (((1,), (1,)), ((), ())), preferred_element_type=f32
                )
                e = jnp.exp(s * (1.0 / SHARP))
                k = e * e
                powered[g, v, at, :] = e.astype(bf16)
                masses[g, v, at, :] = k
                rowsum += fold(e)
                acc[v * COLS + q * 256 : v * COLS + (q + 1) * 256, :] += k[:, :128] + k[:, 128:]
            soft[pl.ds(v * G + g, 1), :] = jnp.sum(rowsum, 0, keepdims=True)

    members(group)
    if half:
        send_columns(acc, refs[-1])


def rows_kernel(sweep, masses, columns, *refs):
    soft = refs[0] if sweep == 0 else None
    out, wide = refs[-2 if sweep < ITERS - 1 else -3], refs[-1]
    c = 1.0 / (K * fold(columns[...].astype(f32)))
    if sweep == ITERS - 1:
        refs[-2][...] = c
    turned = jnp.concatenate([c] * 16, 0).T
    for i in range(2 * Q):
        wide[i * 128 : (i + 1) * 128, :] = jnp.broadcast_to(turned[:, i : i + 1], (128, 128))
    lines = []
    for v in range(2):

        def eight(s, acc):
            at = pl.multiple_of(s * 8, 8)
            cc = wide[pl.ds(v * COLS + at, 8), :]
            cc = jnp.concatenate([cc, cc], 1)
            return tuple(acc[g] + masses[g, v, pl.ds(at, 8), :] * cc for g in range(G))

        acc = lax.fori_loop(0, COLS // 8, eight, (jnp.zeros((8, U), f32),) * G, unroll=32)
        lines += [jnp.sum(a, 0, keepdims=True) for a in acc]
    if soft is not None:
        lines.append(soft[...])
    out[0] = jnp.concatenate(lines, 0).astype(bf16)
    for i in range(1, G):
        out[i] = out[0]


def row_total(ref, first, n):
    return jnp.sum(ref[:, first : first + n, :].astype(f32), 0)


def columns_kernel(masses, rowmass, columns, acc):
    r = 1.0 / (USERS * row_total(rowmass, 0, 2 * G))
    for v in range(2):
        scale = [jnp.broadcast_to(r[v * G + g : v * G + g + 1, :], (8, U)) for g in range(G)]

        def eight(s, _):
            at = pl.multiple_of(s * 8, 8)
            total = masses[0, v, pl.ds(at, 8), :] * scale[0]
            for g in range(1, G):
                total += masses[g, v, pl.ds(at, 8), :] * scale[g]
            acc[pl.ds(v * COLS + at, 8), :] = total[:, :128] + total[:, 128:]
            return 0

        lax.fori_loop(0, COLS // 8, eight, 0, unroll=32)
    send_columns(acc, columns)


def flat_kernel(proto, flat):
    flat[...] = proto[...].astype(f32).T.astype(bf16)


def slopes_kernel(
    mine,
    other,
    flat,
    powered,
    masses,
    scale,
    first,
    last,
    stay,
    near,
    give_stay,
    give_near,
    parts,
    acc,
    wide,
    ab,
    slopes,
):
    acc[...] = jnp.zeros_like(acc)
    turned = jnp.concatenate([scale[...] * (1.0 / SHARP)] * 16, 0).T
    for i in range(2 * Q):
        wide[i * 128 : (i + 1) * 128, :] = jnp.broadcast_to(turned[:, i : i + 1], (128, 128))
    ab[0 : 2 * G, :] = (1.0 / SHARP) / row_total(first, 2 * G, 2 * G)
    ab[2 * G :, :] = 1.0 / row_total(last, 0, 2 * G)

    def group(half, r, rows):
        g = place(half, r)
        slot = ((r << 1) & 3) ^ ((r >> 1) * 3)
        slope = slopes.at[r % 2]
        for v in range(2):
            w = 1 - v
            a = ab[pl.ds(v * G + g, 1), :]
            b = ab[pl.ds(2 * G + w * G + g, 1), :]
            for q in range(Q):
                at = slice(q * 128, (q + 1) * 128)
                c = wide[(w * Q + q) * 128 : (w * Q + q + 1) * 128, :]
                slope[at, v * U : (v + 1) * U] = (
                    powered[g, v, at, :].astype(f32) * a
                    - masses[g, w, at, :] * jnp.concatenate([c, c], 1) * b
                ).astype(bf16)
        made = jnp.dot(flat[...], slope[...], preferred_element_type=f32).astype(bf16)
        for v in range(2):
            out = (give_stay, give_near) if half else (stay, near)
            out[slot // 2][v, slot % 2] = made[:, v * U : (v + 1) * U]
        acc[...] += jnp.dot(slope[...], rows[r].reshape(2 * U, 128), preferred_element_type=f32)

    for half, rows in enumerate((mine, other)):
        for r in range(NX):
            group(half, r, rows)
    for i, (y, z) in enumerate(order(("y", "z"))):
        at = (z - GATHER_FIRST["z"]) % NZ * SUB + y * 8
        parts[i * 8 : (i + 1) * 8, :] = acc[at : at + 8, :]


def piece_kernel(pieces, out):
    out[...] = jnp.concatenate([fold(pieces[...])] * (NY * NX), 0).astype(bf16)


def add_kernel(mine, got, out):
    out[...] = (mine[...].astype(f32) + got[...].astype(f32)).astype(bf16)


def near_kernel(stay, other, got, unit, far):
    for v in range(2):
        unit[v] = stay[v, 0].astype(f32) + other[v, 0].astype(f32) + got[v, 0].astype(f32)
        last = stay[v, 1].astype(f32) + other[v, 1].astype(f32) + got[v, 1].astype(f32)
        far[v] = last.astype(bf16)


def finish_kernel(embeddings, inverse, kept, got, proto, grad_embed, grad_proto):
    for v in range(2):
        grad = (kept[v] + got[v].astype(f32)).T
        inv = inverse[v]
        unit = embeddings[v].astype(f32) * inv
        grad_embed[v] = inv * (grad - unit * jnp.sum(unit * grad, -1, keepdims=True))
    for x in range(NX):
        blocks = []
        for c in range(NC):
            b = proto[c].astype(f32).reshape(NY, NX, 8, 128)[:, (x - FIRST["x"]) % NX]
            blocks += [b[(y - FIRST["y"]) % NY] for y in range(NY)]
        whole = jnp.concatenate(blocks, 0)
        grad_proto[:, x * NC * SUB : (x + 1) * NC * SUB] = whole.T


def swap(x, axis, n, bit):
    return lax.ppermute(x, axis, [(i, i ^ bit) for i in range(n)])


def body(embeddings, prototypes):
    kept = lambda dtype: shape((G, 2, COLS, U), dtype)
    sums = shape((NY * NZ * 8, 128), bf16)
    acc = pltpu.VMEM((2 * COLS, 128), f32)

    unit, inverse, proto = pl.pallas_call(
        prepare_kernel,
        out_shape=(
            shape((2, U, 128), bf16),
            shape((2, U, 1), f32),
            shape((NZ, SUB, 128), bf16),
        ),
        in_specs=[pl.BlockSpec(memory_space=pltpu.HBM)] * 2,
        out_specs=(VM, VM, pl.BlockSpec(memory_space=pl.ANY)),
        scratch_shapes=[
            pltpu.VMEM((2, U, 128), bf16),
            pltpu.VMEM((128, 128), bf16),
            pltpu.VMEM((128, 128), f32),
            pltpu.VMEM((NZ, SUB, 128), bf16),
            pltpu.SemaphoreType.DMA((3,)),
        ],
        compiler_params=pltpu.CompilerParams(vmem_limit_bytes=20 * 1024 * 1024),
    )(*(pltpu.with_memory_space_constraint(a, pltpu.HBM) for a in (embeddings, prototypes)))
    proto = exchange(proto, ("z",), GATHER_FIRST).reshape(COLS, 128)
    others = [swap(unit, "x", NX, r) for r in range(1, NX)]
    flat = call(flat_kernel, shape((128, COLS), bf16), proto, flops=1 << 36)
    others, proto, flat = lax.optimization_barrier((others, proto, flat))
    mine = jnp.stack([unit] + others)
    other = swap(mine, "c", NC, 1)
    part = shape((2 * COLS, 128), f32)
    grid = (kept(bf16), kept(f32), shape((2 * G, U), f32))
    half = call(
        functools.partial(scores_kernel, 0),
        (*grid, part),
        mine,
        proto,
        flops=1 << 31,
    )
    powered, masses, soft, _, columns = call(
        functools.partial(scores_kernel, 1),
        (*grid, part, sums),
        other,
        proto,
        *half,
        aliases={2: 0, 3: 1, 4: 2, 5: 3},
    )
    first = None
    for sweep in range(ITERS):
        columns = exchange(columns, ("y", "z"))
        lines = shape((G, 4 * G if sweep == 0 else 2 * G, U), bf16)
        mass = call(
            functools.partial(rows_kernel, sweep),
            (lines, shape((8, 128), f32)) if sweep == ITERS - 1 else lines,
            masses,
            columns,
            *((soft,) if sweep == 0 else ()),
            scratch=[acc],
        )
        if sweep == ITERS - 1:
            mass, scale = mass
        mass = exchange(mass, ("x", "c"))
        first = mass if first is None else first
        if sweep < ITERS - 1:
            columns = call(columns_kernel, sums, masses, mass, scratch=[acc])
    half = shape((2, 2, 128, U), bf16)
    stay, near, give_stay, give_near, parts = call(
        slopes_kernel,
        (half, half, half, half, shape((COLS, 128), f32)),
        mine,
        other,
        flat,
        powered,
        masses,
        scale,
        first,
        mass,
        scratch=[
            pltpu.VMEM((COLS, 128), f32),
            acc,
            pltpu.VMEM((4 * G, U), f32),
            pltpu.VMEM((2, COLS, 2 * U), bf16),
        ],
    )
    pieces = exchange(parts, ("y", "z"))
    near = call(add_kernel, half, near, swap(give_near, "c", NC, 1))
    other = swap(give_stay, "c", NC, 1)
    near = swap(near, "x", NX, 1)
    pieces = call(piece_kernel, shape((NY * NX * 8, 128), bf16), pieces, flops=1 << 36)
    whole = exchange(pieces, ("y", "x"))
    whole = lax.all_gather(whole, "c", axis=0)
    unit, far = call(
        near_kernel, (shape((2, 128, U), f32), shape((2, 128, U), bf16)), stay, other, near
    )
    far = swap(far, "x", NX, 3)
    return tuple(
        call(
            finish_kernel,
            (shape((2, U, 128), f32), shape((128, COLS), f32)),
            embeddings,
            inverse,
            unit,
            far,
            whole,
        )
    )


def solution(mesh):
    fine = Mesh(mesh.devices.reshape(NY, NX, NC, NZ), ("y", "x", "c", "z"))
    placed = (P(None, ("y", "x", "c", "z"), None), P(None, "z"))
    return jax.shard_map(
        body, mesh=fine, in_specs=placed, out_specs=placed, check_vma=False
    )
```
